128 devices in a mesh: sub: 4 (over y_lo, core), pul: 32 (over y_hi, z, x).
Axes of the slice: x: 4, y: 4 (y_hi: 2, y_lo: 2; y = y_hi * 2 + y_lo), z: 4, core: 2. Of those that a mesh axis runs over, the one named last changes fastest.
Arguments:
- raw_echo: bfloat16 [2, 4, 4096, 16384], P(None, 'sub', None, 'pul'), may hold values from -3 to 3
- range_phase: float32 [4096], replicated, may hold values from -3.140625 to 3.140625
- kappa: float32 [4096], P('pul'), may hold values from 0.5 to 4
- doppler: float32 [4, 16384], replicated, may hold values from -3.140625 to 3.140625
- migration: int32 [128, 16384], P('pul'), may hold values from 0 to 8, as said below
Outputs:
- image: bfloat16 [2, 4096, 16384], P(None, 'pul', 'sub')
The draws below stay inside these ranges and needn't reach their ends.
Inputs may be any that keep to these rules, and one draw needn't show every extreme that they name: `migration`: shifts are whole range bins; the value 8 occurs.
All inputs are finite; a program needn't handle non-finite values.
Results may differ from the reference program's by a relative error of at most 0.02.
Values may be sent and summed in bfloat16 or wider, within the bound.
No kernel may reach another device: no remote copies, remote signals or barrier semaphores. Data moves between devices by JAX's collectives and lax.ppermute only.
A program may use at most 192 MiB of HBM per device.

```python
import math
import jax
import jax.numpy as jnp
from jax import lax

NR = 4096
MAXS = 8
RBLK = 32
NA = 16384
SUBS = 4


def draw_migration(key, part):
    key = jax.random.fold_in(key, 7)
    shifts = jax.random.randint(key, (NR // RBLK, NA), 0, MAXS + 1, dtype=jnp.int32)
    peak_key = jax.random.fold_in(key, 11)
    peak_spot = jax.random.randint(peak_key, (), 0, NR // RBLK * NA, dtype=jnp.int32)
    flat_shifts = shifts.reshape(-1).at[peak_spot].set(MAXS)
    return flat_shifts.reshape(NR // RBLK, NA)


def levels(stream_key, extent, split, smallest, top_value):
    level, own = 1.0, jax.random.fold_in(stream_key, 6)
    for axis_at, blocks in split:
        heights = jnp.exp(jax.random.uniform(jax.random.fold_in(own, axis_at), (blocks,), jnp.float32, smallest / len(split), top_value / len(split)))
        level = level * jnp.repeat(heights, extent[axis_at] // blocks).reshape([-1 if axis == axis_at else 1 for axis in range(len(extent))])
    return level


def centred(rng, extent, scale, reach, cuts=(), kind=jnp.bfloat16):
    values = jax.random.normal(rng, extent, jnp.float32) * scale
    if len(cuts) > 0:
        values = levels(rng, extent, cuts, -0.22, 0.18) * values
    return jnp.clip(values, min=-reach, max=reach).astype(kind)


def setup_inputs(seed: int = 0) -> dict:
    streams_of = jax.random.split(jax.random.key(seed), 6)
    raw_echo = centred(streams_of[0], (2, SUBS, NR, NA), 0.5, 3.0, ((1, 4), (3, 32)))
    range_phase = jnp.clip(jax.random.uniform(streams_of[1], (NR,), jnp.float32, -3.140625, 3.140625), -3.140625, 3.140625)
    kappa = jnp.clip(jnp.exp(math.log(4.0) - 2.0794415 * jax.random.uniform(streams_of[2], (NR,), jnp.float32) ** levels(streams_of[2], (NR,), ((0, 32),), -0.2, 0.2)), 0.5, 4.0)
    doppler = jnp.clip(jax.random.uniform(streams_of[3], (SUBS, NA), jnp.float32, -3.140625, 3.140625), -3.140625, 3.140625)
    migration = draw_migration(jax.random.fold_in(streams_of[5], 71), 0)
    return dict(raw_echo=raw_echo, range_phase=range_phase, kappa=kappa, doppler=doppler, migration=migration)


def factor_pair(length):
    inner_len = 1
    for candidate in range(1, math.isqrt(length) + 1):
        if length % candidate == 0:
            inner_len = candidate
    return (inner_len, length // inner_len)

def fourier_table(length, direction):
    indices = jnp.arange(length, dtype=jnp.int32)
    product = indices[:, None] * indices[None, :] % length
    angles = direction * 2.0 * math.pi / length * product.astype(jnp.float32)
    cosine = jnp.cos(angles)
    sine_part = jnp.sin(angles)
    upper_half = jnp.stack([cosine, -sine_part], axis=1)
    lower_half = jnp.stack([sine_part, cosine], axis=1)
    return jnp.stack([upper_half, lower_half], axis=0).astype(jnp.bfloat16)

def twiddle(outer_len, inner_len, direction):
    length = outer_len * inner_len
    row_ids = jnp.arange(outer_len, dtype=jnp.int32)[:, None]
    col_ids = jnp.arange(inner_len, dtype=jnp.int32)[None, :]
    angles = direction * 2.0 * math.pi / length * (row_ids * col_ids % length).astype(jnp.float32)
    scaling = 1.0 / math.sqrt(length)
    return (jnp.cos(angles) * scaling, jnp.sin(angles) * scaling)

def complex_times(pair, cosine, sine_part):
    real_part = pair[0] * cosine - pair[1] * sine_part
    imag_part = pair[0] * sine_part + pair[1] * cosine
    return jnp.stack([real_part, imag_part], axis=0)

def contract(pattern, table, values):
    return jnp.einsum(pattern, table.astype(jnp.float32), values.astype(jnp.float32), precision=lax.Precision.HIGHEST)

def forward_steps(values, outer_len, inner_len):
    lead_len = values.shape[1]
    tail_len = values.shape[3]
    grid_view = values.reshape(2, lead_len, outer_len, inner_len, tail_len)
    first_pass = contract('dkcm,camib->dakib', fourier_table(outer_len, -1), grid_view)
    cosine, sine_part = twiddle(outer_len, inner_len, -1)
    middle = complex_times(first_pass, cosine[:, :, None], sine_part[:, :, None]).astype(jnp.bfloat16)
    return contract('dkcm,caqmb->daqkb', fourier_table(inner_len, -1), middle)

def backward_steps(spectrum):
    lead_len, outer_len, inner_len, tail_len = (spectrum.shape[1], spectrum.shape[2], spectrum.shape[3], spectrum.shape[4])
    first_pass = contract('dkcm,caqmb->daqkb', fourier_table(inner_len, 1), spectrum)
    cosine, sine_part = twiddle(outer_len, inner_len, 1)
    middle = complex_times(first_pass, cosine[:, :, None], sine_part[:, :, None]).astype(jnp.bfloat16)
    result = contract('dkcm,camib->dakib', fourier_table(outer_len, 1), middle)
    return result.reshape(2, lead_len, outer_len * inner_len, tail_len)

def reference(raw_echo, range_phase, kappa, doppler, migration):
    range_inner, range_outer = factor_pair(NR)
    pulse_inner, pulse_outer = factor_pair(NA)
    range_cos = jnp.cos(range_phase)[None, :, None]
    range_sin = jnp.sin(range_phase)[None, :, None]
    source_rows = jnp.repeat(migration, RBLK, axis=0) + jnp.arange(NR, dtype=jnp.int32)[:, None]
    gather_index = jnp.broadcast_to(source_rows[None], (2, NR, NA)).astype(jnp.int32)
    zero_rim = jnp.zeros((2, MAXS, NA), jnp.bfloat16)

    def one_aperture(aperture, total):
        samples = lax.dynamic_index_in_dim(raw_echo, aperture, 1, keepdims=False)[:, None]
        freq_perm = forward_steps(samples, range_outer, range_inner)
        freq_nat = jnp.swapaxes(freq_perm, 2, 3).reshape(2, 1, NR, NA)
        ranged = complex_times(freq_nat, range_cos, range_sin).astype(jnp.bfloat16)
        ranged_perm = jnp.swapaxes(ranged.reshape(2, 1, range_inner, range_outer, NA), 2, 3)
        compressed = backward_steps(ranged_perm).astype(jnp.bfloat16)
        spec_perm = forward_steps(compressed.reshape(2, NR, NA, 1), pulse_outer, pulse_inner)
        spectrum = jnp.swapaxes(spec_perm, 2, 3).reshape(2, NR, NA).astype(jnp.bfloat16)
        padded = jnp.concatenate([spectrum, zero_rim], axis=1)
        shifted = jnp.take_along_axis(padded, gather_index, axis=1)
        doppler_row = lax.dynamic_index_in_dim(doppler, aperture, 0, keepdims=False)
        phases = kappa[:, None] * doppler_row[None, :]
        filtered = complex_times(shifted.astype(jnp.float32), jnp.cos(phases), jnp.sin(phases)).astype(jnp.bfloat16)
        filtered_perm = jnp.swapaxes(filtered.reshape(2, NR, pulse_inner, pulse_outer, 1), 2, 3)
        sub_image = backward_steps(filtered_perm).reshape(2, NR, NA).astype(jnp.bfloat16)
        return total + sub_image.astype(jnp.float32)
    total = lax.fori_loop(0, SUBS, one_aperture, jnp.zeros((2, NR, NA), jnp.float32))
    return total.astype(jnp.bfloat16)
```

```python
import functools
import math

import jax
import jax.numpy as jnp
import numpy as np
from jax import lax
from jax.experimental import pallas as pl
from jax.experimental.pallas import tpu as pltpu
from jax.sharding import PartitionSpec as P

MAXS = 8
RBLK = 32
LANES = 128
CHUNKS = 2
VMEM = 56 * 1024 * 1024
F32 = jnp.float32
BF16 = jnp.bfloat16


def realified(table):
    return np.block([[table.real, -table.imag], [table.imag, table.real]])


def unit_table(rows, cols, length, direction):
    product = np.outer(np.asarray(rows), np.asarray(cols)) % length
    return np.exp(direction * 2j * np.pi * product / length)


def as_bf16(table):
    return np.asarray(table, np.float32).astype(BF16)


def range_middle(range_phase, size):
    length = size * size
    k2 = np.arange(size)[:, None, None]
    j1 = np.arange(size)[None, :, None]
    k1 = np.arange(size)[None, None, :]
    wave = np.exp(2j * np.pi * ((j1 * (k2 + size * k1)) % length) / length) / size
    wave_r, wave_i = wave.real.astype(np.float32), wave.imag.astype(np.float32)
    right = np.concatenate(
        [
            np.concatenate([wave_r, -wave_i], axis=2),
            np.concatenate([wave_i, wave_r], axis=2),
        ],
        axis=1,
    )
    phase = range_phase.reshape(size, size).T
    cosine, sine = jnp.cos(phase)[:, None, :], jnp.sin(phase)[:, None, :]
    left_r = wave_r * cosine - wave_i * sine
    left_i = wave_r * sine + wave_i * cosine
    left = jnp.concatenate(
        [
            jnp.concatenate([left_r, -left_i], axis=2),
            jnp.concatenate([left_i, left_r], axis=2),
        ],
        axis=1,
    ).astype(BF16)
    middle = jnp.einsum("kae,kbe->kab", left, as_bf16(right), preferred_element_type=F32)
    return middle.astype(BF16)


def range_kernel(size, x_ref, w_ref, t_ref, v_ref, o_ref, one, two):
    length = size * size
    halves = x_ref.shape[2] // LANES
    both = 2 * size

    def cast(step, carry):
        for h in range(halves):
            for c in range(2):
                one[h, pl.ds(c * length + 128 * step, 128), :] = x_ref[
                    c, pl.ds(pl.multiple_of(128 * step, 128), 128), h * LANES : (h + 1) * LANES
                ].astype(F32)
        return carry

    lax.fori_loop(0, length // 128, cast, 0)

    def strided(source, target, table):
        def body(step, carry):
            for u in range(4):
                j1 = step * 4 + u
                value = jnp.concatenate(
                    [source[h, pl.ds(j1, both, stride=size), :] for h in range(halves)], axis=1
                ).astype(BF16)
                out = jnp.dot(table, value, preferred_element_type=F32)
                for h in range(halves):
                    target[h, pl.ds(j1, both, stride=size), :] = out[
                        :, h * LANES : (h + 1) * LANES
                    ]
            return carry

        lax.fori_loop(0, size // 4, body, 0)

    strided(one, two, w_ref[...])

    def inner(step, carry):
        for u in range(4):
            k2 = step * 4 + u
            value = jnp.concatenate(
                [
                    jnp.concatenate(
                        [
                            two[h, pl.ds(pl.multiple_of((c * size + k2) * size, size), size), :]
                            for c in range(2)
                        ],
                        axis=0,
                    )
                    for h in range(halves)
                ],
                axis=1,
            ).astype(BF16)
            out = jnp.dot(t_ref[k2], value, preferred_element_type=F32)
            for h in range(halves):
                for d in range(2):
                    one[h, pl.ds(pl.multiple_of((d * size + k2) * size, size), size), :] = out[
                        d * size : (d + 1) * size, h * LANES : (h + 1) * LANES
                    ]
        return carry

    lax.fori_loop(0, size // 4, inner, 0)
    strided(one, two, v_ref[...])
    blocks, rows = o_ref.shape[0], o_ref.shape[2]

    def give(step, carry):
        for u in range(4):
            block = step * 4 + u
            for d in range(2):
                for h in range(halves):
                    o_ref[block, d, :, h * LANES : (h + 1) * LANES] = two[
                        h, pl.ds(pl.multiple_of(d * length + block * rows, rows), rows), :
                    ].astype(BF16)
        return carry

    lax.fori_loop(0, blocks // 4, give, 0)


def range_compress(echo, middle, chunk, width, blocks):
    length = echo.shape[1]
    size = math.isqrt(length)
    index = np.arange(size)
    forward = as_bf16(realified(unit_table(index, index, size, -1)))
    backward = as_bf16(realified(unit_table(index, index, size, 1)))
    rows = length // blocks
    whole = lambda *shape: pl.BlockSpec(shape, lambda i: (0,) * len(shape))
    return pl.pallas_call(
        functools.partial(range_kernel, size),
        grid=(1,),
        in_specs=[
            pl.BlockSpec((2, length, width), lambda i: (0, 0, chunk)),
            whole(2 * size, 2 * size),
            whole(size, 2 * size, 2 * size),
            whole(2 * size, 2 * size),
        ],
        out_specs=whole(blocks, 2, rows, width),
        out_shape=jax.ShapeDtypeStruct((blocks, 2, rows, width), BF16),
        scratch_shapes=[
            pltpu.VMEM((width // LANES, 2 * length, LANES), F32),
            pltpu.VMEM((width // LANES, 2 * length, LANES), F32),
        ],
        compiler_params=pltpu.CompilerParams(vmem_limit_bytes=VMEM),
        name="range_compress",
    )(echo, forward, middle, backward)


def doppler_kernel(rows, *refs):
    parts = refs[:CHUNKS]
    w_ref, cos_ref, sin_ref, u_ref, o_ref, held = refs[CHUNKS:]
    sources = parts[0].shape[0]
    halves = parts[0].shape[4] // LANES
    size = cos_ref.shape[0]

    def cast(source, carry):
        for q in range(CHUNKS):
            for c in range(2):
                for h in range(halves):
                    base = ((c * CHUNKS + q) * halves + h) * sources
                    held[pl.ds(pl.multiple_of((base + source) * rows, rows), rows), :] = parts[q][
                        source, 0, c, :, h * LANES : (h + 1) * LANES
                    ].astype(F32)
        return carry

    lax.fori_loop(0, sources, cast, 0)

    def body(step, carry):
        pair = [step * 2, step * 2 + 1]
        value = jnp.concatenate(
            [held[pl.ds(row, 2 * size, stride=rows), :] for row in pair], axis=1
        ).astype(BF16)
        first = jnp.dot(w_ref[...], value, preferred_element_type=F32)
        stacked = []
        for i in range(2):
            real = first[:size, i * LANES : (i + 1) * LANES]
            imag = first[size:, i * LANES : (i + 1) * LANES]
            stacked.append(
                jnp.concatenate(
                    [
                        real * cos_ref[...] - imag * sin_ref[...],
                        real * sin_ref[...] + imag * cos_ref[...],
                    ],
                    axis=1,
                ).astype(BF16)
            )
        second = jnp.dot(
            jnp.concatenate(stacked, axis=0), u_ref[...], preferred_element_type=F32
        ).astype(BF16)
        for i in range(2):
            for d in range(2):
                o_ref[0, pair[i], d] = second[i * size : (i + 1) * size, d * LANES : (d + 1) * LANES]
        return carry

    lax.fori_loop(0, rows // 2, body, 0)


def doppler_tables(size, direction):
    index = np.arange(size)
    table = unit_table(index, index, size, direction)
    turn = unit_table(index, index, size * size, direction) / size
    return table, turn.real.astype(np.float32), turn.imag.astype(np.float32)


def doppler_forward(parts, part, rows, size):
    sources, subs, _, _, width = parts[0].shape
    halves = width // LANES
    table, turn_cos, turn_sin = doppler_tables(size, -1)
    per_source = size // sources
    order = np.asarray(
        [
            per_source * source + q * halves + h
            for q in range(CHUNKS)
            for h in range(halves)
            for source in range(sources)
        ]
    )
    outer = as_bf16(realified(table[:, order]))
    inner = as_bf16(realified(table).T)
    whole = lambda *shape: pl.BlockSpec(shape, lambda i: (0,) * len(shape))
    piece = pl.BlockSpec((sources, 1, 2, rows, width), lambda i: (0, i, 0, part, 0))
    return pl.pallas_call(
        functools.partial(doppler_kernel, rows),
        grid=(subs,),
        in_specs=[piece] * CHUNKS
        + [
            whole(2 * size, 2 * size),
            whole(size, size),
            whole(size, size),
            whole(2 * size, 2 * size),
        ],
        out_specs=pl.BlockSpec((1, rows, 2, size, size), lambda i: (i, 0, 0, 0, 0)),
        out_shape=jax.ShapeDtypeStruct((subs, rows, 2, size, size), BF16),
        scratch_shapes=[pltpu.VMEM((2 * size * rows, LANES), F32)],
        compiler_params=pltpu.CompilerParams(vmem_limit_bytes=VMEM),
        name="doppler_forward",
    )(*parts, outer, turn_cos, turn_sin, inner)


def turn_polynomials():
    nodes = 0.25 * (1 - np.cos((np.arange(64) + 0.5) * np.pi / 64)) / 2
    roots = np.sqrt(nodes)
    sine = np.polynomial.polynomial.polyfit(nodes, np.sin(2 * np.pi * roots) / roots, 6)
    cosine = np.polynomial.polynomial.polyfit(nodes, np.cos(2 * np.pi * roots), 6)
    return [round(float(v), 7) for v in sine], [round(float(v), 7) for v in cosine]


def turns(cycles):
    sine_terms, cosine_terms = turn_polynomials()
    part = cycles - jnp.floor(cycles + 0.5)
    square = part * part
    sine = jnp.full_like(square, sine_terms[-1])
    cosine = jnp.full_like(square, cosine_terms[-1])
    for term in reversed(sine_terms[:-1]):
        sine = sine * square + term
    for term in reversed(cosine_terms[:-1]):
        cosine = cosine * square + term
    return cosine, sine * part


def image_kernel(kappa_ref, *refs):
    low, high, rim, shift_ref, phase_ref, w_ref, cos_ref, sin_ref, u_ref, o_ref = refs[:10]
    moved, summed, middle, turned = refs[10:]
    step = pl.program_id(0)
    subs, half = low.shape[0], low.shape[1]
    rows = 2 * half
    tile = low.shape[3]
    size = w_ref.shape[0] // 2
    shift = shift_ref[...]
    bits = [(shift & 1) > 0, (shift & 2) > 0, (shift & 4) > 0, (shift & 8) > 0]

    def aperture(index, carry):
        for d in range(2):
            values = [low[index, r, d].astype(F32) for r in range(half)]
            values += [high[index, r, d].astype(F32) for r in range(half)]
            values += [rim[index, r, d].astype(F32) for r in range(MAXS)]
            four = [jnp.where(bits[2], values[r + 4], values[r]) for r in range(rows + 3)]
            two = [jnp.where(bits[1], four[r + 2], four[r]) for r in range(rows + 1)]
            one = [jnp.where(bits[0], two[r + 1], two[r]) for r in range(rows)]
            for r in range(rows):
                moved[index, d, r] = jnp.where(bits[3], values[r + 8], one[r])
        return carry

    lax.fori_loop(0, subs, aperture, 0)

    def row_sum(row, carry):
        factor = kappa_ref[row]
        real = jnp.zeros((tile, size), F32)
        imag = jnp.zeros((tile, size), F32)
        for index in range(subs):
            cosine, sine = turns(factor * phase_ref[index])
            a, b = moved[index, 0, row], moved[index, 1, row]
            real = real + (a * cosine - b * sine)
            imag = imag + (a * sine + b * cosine)
        summed[pl.ds(pl.multiple_of(row * tile, tile), tile), :] = jnp.concatenate(
            [real, imag], axis=1
        ).astype(BF16)
        return carry

    lax.fori_loop(0, rows, row_sum, 0)
    first = jnp.dot(summed[...], u_ref[...], preferred_element_type=F32)
    for r in range(rows):
        real = first[r * tile : (r + 1) * tile, :size]
        imag = first[r * tile : (r + 1) * tile, size:]
        where = pl.ds(pl.multiple_of(step * tile, tile), tile)
        middle[r, 0, where, :] = (real * cos_ref[...] - imag * sin_ref[...]).astype(BF16)
        middle[r, 1, where, :] = (real * sin_ref[...] + imag * cos_ref[...]).astype(BF16)

    @pl.when(step == pl.num_programs(0) - 1)
    def _():
        def body(pair, carry):
            value = jnp.concatenate(
                [
                    jnp.concatenate([middle[pair * 2 + i, c] for c in range(2)], axis=0)
                    for i in range(2)
                ],
                axis=1,
            )
            out = jnp.dot(w_ref[...], value, preferred_element_type=F32)
            for i in range(2):
                turned[pl.ds(pair * 2 + i, 2 * size, stride=rows), :] = out[
                    :, i * LANES : (i + 1) * LANES
                ]
            return carry

        lax.fori_loop(0, rows // 2, body, 0)
        groups = o_ref.shape[0]
        per_group = size // groups

        def give(group, carry):
            for d in range(2):
                for j in range(per_group):
                    line = (d * size + group * per_group + j) * rows
                    o_ref[group, d, :, j * LANES : (j + 1) * LANES] = turned[
                        pl.ds(pl.multiple_of(line, rows), rows), :
                    ].astype(BF16)
            return carry

        lax.fori_loop(0, groups, give, 0)


def image_rows(kappa, low, high, rim, shift, phase, groups):
    subs, half, _, size, _ = low.shape
    rows = 2 * half
    tile = 16
    table, turn_cos, turn_sin = doppler_tables(size, 1)
    outer = as_bf16(realified(table))
    inner = as_bf16(realified(table).T)
    whole = lambda *shape: pl.BlockSpec(shape, lambda i: (0,) * len(shape))
    lines = pl.BlockSpec((tile, size), lambda i: (i, 0))
    width = size * size // groups
    return pl.pallas_call(
        image_kernel,
        grid=(size // tile,),
        in_specs=[
            pl.BlockSpec(memory_space=pltpu.SMEM),
            pl.BlockSpec((subs, half, 2, tile, size), lambda i: (0, 0, 0, i, 0)),
            pl.BlockSpec((subs, half, 2, tile, size), lambda i: (0, 0, 0, i, 0)),
            pl.BlockSpec((subs, MAXS, 2, tile, size), lambda i: (0, 0, 0, i, 0)),
            lines,
            pl.BlockSpec((subs, tile, size), lambda i: (0, i, 0)),
            whole(2 * size, 2 * size),
            lines,
            lines,
            whole(2 * size, 2 * size),
        ],
        out_specs=whole(groups, 2, rows, width),
        out_shape=jax.ShapeDtypeStruct((groups, 2, rows, width), BF16),
        scratch_shapes=[
            pltpu.VMEM((subs, 2, rows, tile, size), F32),
            pltpu.VMEM((rows * tile, 2 * size), BF16),
            pltpu.VMEM((rows, 2, size, size), BF16),
            pltpu.VMEM((2 * size * rows, LANES), F32),
        ],
        compiler_params=pltpu.CompilerParams(vmem_limit_bytes=VMEM),
        name="image_rows",
    )(kappa, low, high, rim, shift, phase, outer, turn_cos, turn_sin, inner)


def on_device(raw_echo, range_phase, kappa, doppler, migration):
    _, _, range_len, pulse_dev = raw_echo.shape
    puls, subs = lax.axis_size("pul"), lax.axis_size("sub")
    blocks = puls * subs
    rows = range_len // blocks
    pulse_len = pulse_dev * puls
    size = math.isqrt(pulse_len)
    sub_index = lax.axis_index("sub")
    middle = range_middle(range_phase, math.isqrt(range_len))
    echo = raw_echo.reshape(2, range_len, pulse_dev)
    width = pulse_dev // CHUNKS
    parts = []
    for chunk in range(CHUNKS):
        sent = range_compress(echo, middle, chunk, width, blocks)
        got = lax.all_to_all(sent, ("pul", "sub"), 0, 0, tiled=True)
        parts.append(got.reshape(puls, subs, 2, rows, width))
    own_shift = lax.dynamic_slice_in_dim(migration, sub_index, 1, 0)
    shift = own_shift.reshape(size, size).T
    phase = jnp.swapaxes(doppler.reshape(subs, size, size), 1, 2) * (0.5 / math.pi)
    own_kappa = lax.dynamic_slice_in_dim(kappa, sub_index * rows, rows, 0)
    half = rows // 2
    low = doppler_forward(parts, 0, half, size)
    place = lambda block: (block % subs) * puls + block // subs
    pairs = [(place(block), place(block - 1)) for block in range(1, blocks)]
    rim = lax.ppermute(low[:, :MAXS], ("sub", "pul"), pairs)
    high = doppler_forward(parts, 1, half, size)
    sent = image_rows(own_kappa, low, high, rim, shift, phase, subs)
    return lax.all_to_all(sent, "sub", 0, 2, tiled=True).reshape(2, rows * subs, pulse_len // subs)


def solution(mesh):
    placed = (P(None, "sub", None, "pul"), P(), P("pul"), P(), P("pul", None))
    return jax.shard_map(
        on_device, mesh=mesh, in_specs=placed, out_specs=P(None, "pul", "sub"), check_vma=False
    )
```

```python
import functools
import math

import jax
import jax.numpy as jnp
import numpy as np
from jax import lax
from jax.experimental import pallas as pl
from jax.experimental.pallas import tpu as pltpu
from jax.sharding import PartitionSpec as P

MAXS = 8
RBLK = 32
LANES = 128
CHUNKS = 2
UNROLL = 8
VMEM = 56 * 1024 * 1024
F32 = jnp.float32
BF16 = jnp.bfloat16


def realified(table):
    return np.block([[table.real, -table.imag], [table.imag, table.real]])


def unit_table(rows, cols, length, direction):
    product = np.outer(np.asarray(rows), np.asarray(cols)) % length
    return np.exp(direction * 2j * np.pi * product / length)


def as_bf16(table):
    return np.asarray(table, np.float32).astype(BF16)


def range_middle(range_phase, size):
    length = size * size
    k2 = np.arange(size)[:, None, None]
    j1 = np.arange(size)[None, :, None]
    k1 = np.arange(size)[None, None, :]
    wave = np.exp(2j * np.pi * ((j1 * (k2 + size * k1)) % length) / length) / size
    wave_r, wave_i = wave.real.astype(np.float32), wave.imag.astype(np.float32)
    right = np.concatenate(
        [
            np.concatenate([wave_r, -wave_i], axis=2),
            np.concatenate([wave_i, wave_r], axis=2),
        ],
        axis=1,
    )
    phase = range_phase.reshape(size, size).T
    cosine, sine = jnp.cos(phase)[:, None, :], jnp.sin(phase)[:, None, :]
    left_r = wave_r * cosine - wave_i * sine
    left_i = wave_r * sine + wave_i * cosine
    left = jnp.concatenate(
        [
            jnp.concatenate([left_r, -left_i], axis=2),
            jnp.concatenate([left_i, left_r], axis=2),
        ],
        axis=1,
    ).astype(BF16)
    middle = jnp.einsum("kae,kbe->kab", left, as_bf16(right), preferred_element_type=F32)
    return middle.astype(BF16)


def range_kernel(size, splits, x_ref, w_ref, t_ref, v_ref, *refs):
    outs, (one, two) = refs[:splits], refs[splits:]
    halves = x_ref.shape[2] // LANES
    both = 2 * size
    pitch = size + 1

    def lanes(h):
        return slice(h * LANES, (h + 1) * LANES)

    def cast(step, carry):
        for u in range(4):
            line = step * 4 + u
            for h in range(halves):
                for c in range(2):
                    one[h, pl.ds((c * size + line) * pitch, size), :] = x_ref[
                        c, pl.ds(pl.multiple_of(line * size, size), size), lanes(h)
                    ].astype(F32)
        return carry

    lax.fori_loop(0, size // 4, cast, 0)

    def strided(source, target, table):
        def body(step, carry):
            for u in range(UNROLL):
                j1 = step * UNROLL + u
                value = jnp.concatenate(
                    [source[h, pl.ds(j1, both, stride=pitch), :] for h in range(halves)], axis=1
                ).astype(BF16)
                out = jnp.dot(table, value, preferred_element_type=F32)
                for h in range(halves):
                    target[h, pl.ds(j1, both, stride=pitch), :] = out[:, lanes(h)]
            return carry

        lax.fori_loop(0, size // UNROLL, body, 0)

    strided(one, two, w_ref[...])

    def inner(step, carry):
        for u in range(UNROLL):
            k2 = step * UNROLL + u
            value = jnp.concatenate(
                [
                    jnp.concatenate(
                        [two[h, pl.ds((c * size + k2) * pitch, size), :] for c in range(2)], axis=0
                    )
                    for h in range(halves)
                ],
                axis=1,
            ).astype(BF16)
            out = jnp.dot(t_ref[k2], value, preferred_element_type=F32)
            for h in range(halves):
                for d in range(2):
                    one[h, pl.ds((d * size + k2) * pitch, size), :] = out[
                        d * size : (d + 1) * size, lanes(h)
                    ]
        return carry

    lax.fori_loop(0, size // UNROLL, inner, 0)
    strided(one, two, v_ref[...])
    rows = outs[0].shape[2]
    pieces = size // rows

    def give(step, carry):
        for u in range(4):
            line = step * 4 + u
            for piece in range(pieces):
                block = line * (pieces // splits) + piece // splits
                for d in range(2):
                    for h in range(halves):
                        outs[piece % splits][block, d, :, lanes(h)] = two[
                            h, pl.ds((d * size + line) * pitch + piece * rows, rows), :
                        ].astype(BF16)
        return carry

    lax.fori_loop(0, size // 4, give, 0)


def range_compress(echo, middle, chunk, width, blocks, splits):
    length = echo.shape[1]
    size = math.isqrt(length)
    index = np.arange(size)
    forward = as_bf16(realified(unit_table(index, index, size, -1)))
    backward = as_bf16(realified(unit_table(index, index, size, 1)))
    rows = length // blocks // splits
    whole = lambda *shape: pl.BlockSpec(shape, lambda i: (0,) * len(shape))
    scratch = pltpu.VMEM((width // LANES, 2 * (length + size), LANES), F32)
    return pl.pallas_call(
        functools.partial(range_kernel, size, splits),
        grid=(1,),
        in_specs=[
            pl.BlockSpec((2, length, width), lambda i: (0, 0, chunk)),
            whole(2 * size, 2 * size),
            whole(size, 2 * size, 2 * size),
            whole(2 * size, 2 * size),
        ],
        out_specs=[whole(blocks, 2, rows, width)] * splits,
        out_shape=[jax.ShapeDtypeStruct((blocks, 2, rows, width), BF16)] * splits,
        scratch_shapes=[scratch, scratch],
        compiler_params=pltpu.CompilerParams(vmem_limit_bytes=VMEM),
        name="range_compress",
    )(echo, forward, middle, backward)


def doppler_kernel(rows, *refs):
    parts = refs[:CHUNKS]
    w_ref, cos_ref, sin_ref, u_ref, o_ref, held = refs[CHUNKS:]
    sources = parts[0].shape[0]
    halves = parts[0].shape[4] // LANES
    size = cos_ref.shape[0]
    pitch = rows + 1

    def cast(source, carry):
        for q in range(CHUNKS):
            for c in range(2):
                for h in range(halves):
                    base = ((c * CHUNKS + q) * halves + h) * sources
                    held[pl.ds((base + source) * pitch, rows), :] = parts[q][
                        source, 0, c, :, h * LANES : (h + 1) * LANES
                    ].astype(F32)
        return carry

    lax.fori_loop(0, sources, cast, 0)

    def pair(first_row):
        value = jnp.concatenate(
            [held[pl.ds(first_row + i, 2 * size, stride=pitch), :] for i in range(2)], axis=1
        ).astype(BF16)
        first = jnp.dot(w_ref[...], value, preferred_element_type=F32)
        stacked = []
        for i in range(2):
            real = first[:size, i * LANES : (i + 1) * LANES]
            imag = first[size:, i * LANES : (i + 1) * LANES]
            stacked.append(
                jnp.concatenate(
                    [
                        real * cos_ref[...] - imag * sin_ref[...],
                        real * sin_ref[...] + imag * cos_ref[...],
                    ],
                    axis=1,
                ).astype(BF16)
            )
        second = jnp.dot(
            jnp.concatenate(stacked, axis=0), u_ref[...], preferred_element_type=F32
        ).astype(BF16)
        for i in range(2):
            for d in range(2):
                o_ref[0, first_row + i, d] = second[
                    i * size : (i + 1) * size, d * LANES : (d + 1) * LANES
                ]

    def body(step, carry):
        for u in range(4):
            pair(step * 8 + 2 * u)
        return carry

    lax.fori_loop(0, rows // 8, body, 0)


def doppler_tables(size, direction):
    index = np.arange(size)
    table = unit_table(index, index, size, direction)
    turn = unit_table(index, index, size * size, direction) / size
    return table, turn.real.astype(np.float32), turn.imag.astype(np.float32)


def doppler_forward(parts, places, rows, size):
    sources, subs, _, _, width = parts[0].shape
    halves = width // LANES
    table, turn_cos, turn_sin = doppler_tables(size, -1)
    per_source = size // sources
    order = np.asarray(
        [
            per_source * source + q * halves + h
            for q in range(CHUNKS)
            for h in range(halves)
            for source in range(sources)
        ]
    )
    outer = as_bf16(realified(table[:, order]))
    inner = as_bf16(realified(table).T)
    whole = lambda *shape: pl.BlockSpec(shape, lambda i: (0,) * len(shape))
    pieces = [
        pl.BlockSpec(
            (sources, 1, 2, rows, width), functools.partial(lambda at, i: (0, i, 0, at, 0), at)
        )
        for at in places
    ]
    return pl.pallas_call(
        functools.partial(doppler_kernel, rows),
        grid=(subs,),
        in_specs=pieces
        + [
            whole(2 * size, 2 * size),
            whole(size, size),
            whole(size, size),
            whole(2 * size, 2 * size),
        ],
        out_specs=pl.BlockSpec((1, rows, 2, size, size), lambda i: (i, 0, 0, 0, 0)),
        out_shape=jax.ShapeDtypeStruct((subs, rows, 2, size, size), BF16),
        scratch_shapes=[pltpu.VMEM((2 * size * (rows + 1), LANES), F32)],
        compiler_params=pltpu.CompilerParams(vmem_limit_bytes=VMEM),
        name="doppler_forward",
    )(*parts, outer, turn_cos, turn_sin, inner)


def turn_polynomials():
    nodes = 0.25 * (1 - np.cos((np.arange(64) + 0.5) * np.pi / 64)) / 2
    roots = np.sqrt(nodes)
    sine = np.polynomial.polynomial.polyfit(nodes, np.sin(2 * np.pi * roots) / roots, 6)
    cosine = np.polynomial.polynomial.polyfit(nodes, np.cos(2 * np.pi * roots), 6)
    return [round(float(v), 7) for v in sine], [round(float(v), 7) for v in cosine]


def turns(cycles):
    sine_terms, cosine_terms = turn_polynomials()
    part = cycles - jnp.floor(cycles + 0.5)
    square = part * part
    sine = jnp.full_like(square, sine_terms[-1])
    cosine = jnp.full_like(square, cosine_terms[-1])
    for term in reversed(sine_terms[:-1]):
        sine = sine * square + term
    for term in reversed(cosine_terms[:-1]):
        cosine = cosine * square + term
    return cosine, sine * part


def factor_kernel(kappa_ref, phase_ref, o_ref):
    def body(step, carry):
        for u in range(2):
            row = step * 2 + u
            cosine, sine = turns(kappa_ref[row] * phase_ref[0])
            o_ref[0, row, 0] = cosine.astype(BF16)
            o_ref[0, row, 1] = sine.astype(BF16)
        return carry

    lax.fori_loop(0, o_ref.shape[1] // 2, body, 0)


def azimuth_factors(kappa, phase):
    subs, size, _ = phase.shape
    rows = kappa.shape[0]
    return pl.pallas_call(
        factor_kernel,
        grid=(subs,),
        in_specs=[
            pl.BlockSpec(memory_space=pltpu.SMEM),
            pl.BlockSpec((1, size, size), lambda i: (i, 0, 0)),
        ],
        out_specs=pl.BlockSpec((1, rows, 2, size, size), lambda i: (i, 0, 0, 0, 0)),
        out_shape=jax.ShapeDtypeStruct((subs, rows, 2, size, size), BF16),
        compiler_params=pltpu.CompilerParams(vmem_limit_bytes=VMEM),
        name="azimuth_factors",
    )(kappa, phase)


def image_kernel(own, rim, factor_ref, shift_ref, w_ref, cos_ref, sin_ref, u_ref, *refs):
    o_ref, moved, summed, middle, turned = refs
    step = pl.program_id(0)
    subs, rows, _, tile, size = own.shape
    shift = shift_ref[...]
    bits = [((shift >> k) & 1).astype(F32).astype(BF16) > 0.5 for k in range(4)]

    def aperture(index, carry):
        for d in range(2):
            values = [own[index, r, d] for r in range(rows)]
            values += [rim[index, r, d] for r in range(MAXS)]
            four = [jnp.where(bits[2], values[r + 4], values[r]) for r in range(rows + 3)]
            two = [jnp.where(bits[1], four[r + 2], four[r]) for r in range(rows + 1)]
            one = [jnp.where(bits[0], two[r + 1], two[r]) for r in range(rows)]
            for r in range(rows):
                moved[index, d, r] = jnp.where(bits[3], values[r + 8], one[r])
        return carry

    lax.fori_loop(0, subs, aperture, 0)

    def row_sum(turn, carry):
        for u in range(4):
            row = turn * 4 + u
            real = jnp.zeros((tile, size), F32)
            imag = jnp.zeros((tile, size), F32)
            for index in range(subs):
                cosine = factor_ref[index, row, 0].astype(F32)
                sine = factor_ref[index, row, 1].astype(F32)
                a, b = moved[index, 0, row].astype(F32), moved[index, 1, row].astype(F32)
                real = real + (a * cosine - b * sine)
                imag = imag + (a * sine + b * cosine)
            summed[pl.ds(pl.multiple_of(row * tile, tile), tile), :] = jnp.concatenate(
                [real, imag], axis=1
            ).astype(BF16)
        return carry

    lax.fori_loop(0, rows // 4, row_sum, 0)
    first = jnp.dot(summed[...], u_ref[...], preferred_element_type=F32)
    where = pl.ds(pl.multiple_of(step * tile, tile), tile)
    for r in range(rows):
        real = first[r * tile : (r + 1) * tile, :size]
        imag = first[r * tile : (r + 1) * tile, size:]
        middle[r, 0, where, :] = (real * cos_ref[...] - imag * sin_ref[...]).astype(BF16)
        middle[r, 1, where, :] = (real * sin_ref[...] + imag * cos_ref[...]).astype(BF16)

    @pl.when(step == pl.num_programs(0) - 1)
    def _():
        pitch = rows + 1

        def body(turn, carry):
            for u in range(4):
                pair = turn * 4 + u
                value = jnp.concatenate(
                    [
                        jnp.concatenate([middle[pair * 2 + i, c] for c in range(2)], axis=0)
                        for i in range(2)
                    ],
                    axis=1,
                )
                out = jnp.dot(w_ref[...], value, preferred_element_type=F32)
                for i in range(2):
                    turned[pl.ds(pair * 2 + i, 2 * size, stride=pitch), :] = out[
                        :, i * LANES : (i + 1) * LANES
                    ]
            return carry

        lax.fori_loop(0, rows // 8, body, 0)
        groups = o_ref.shape[0]
        per_group = size // groups

        def give(group, carry):
            for d in range(2):
                for j in range(per_group):
                    line = (d * size + group * per_group + j) * pitch
                    o_ref[group, d, :, j * LANES : (j + 1) * LANES] = turned[
                        pl.ds(line, rows), :
                    ].astype(BF16)
            return carry

        lax.fori_loop(0, groups, give, 0)


def image_rows(own, rim, factors, part, shift, groups):
    subs, rows, _, size, _ = own.shape
    tile = 16
    table, turn_cos, turn_sin = doppler_tables(size, 1)
    outer = as_bf16(realified(table))
    inner = as_bf16(realified(table).T)
    whole = lambda *shape: pl.BlockSpec(shape, lambda i: (0,) * len(shape))
    lines = pl.BlockSpec((tile, size), lambda i: (i, 0))
    width = size * size // groups
    return pl.pallas_call(
        image_kernel,
        grid=(size // tile,),
        in_specs=[
            pl.BlockSpec((subs, rows, 2, tile, size), lambda i: (0, 0, 0, i, 0)),
            pl.BlockSpec((subs, MAXS, 2, tile, size), lambda i: (0, 0, 0, i, 0)),
            pl.BlockSpec((subs, rows, 2, tile, size), lambda i: (0, part, 0, i, 0)),
            lines,
            whole(2 * size, 2 * size),
            lines,
            lines,
            whole(2 * size, 2 * size),
        ],
        out_specs=whole(groups, 2, rows, width),
        out_shape=jax.ShapeDtypeStruct((groups, 2, rows, width), BF16),
        scratch_shapes=[
            pltpu.VMEM((subs, 2, rows, tile, size), BF16),
            pltpu.VMEM((rows * tile, 2 * size), BF16),
            pltpu.VMEM((rows, 2, size, size), BF16),
            pltpu.VMEM((2 * size * (rows + 1), LANES), F32),
        ],
        compiler_params=pltpu.CompilerParams(vmem_limit_bytes=VMEM),
        name="image_rows",
    )(own, rim, factors, shift, outer, turn_cos, turn_sin, inner)


def on_device(raw_echo, range_phase, kappa, doppler, migration):
    _, _, range_len, pulse_dev = raw_echo.shape
    puls, subs = lax.axis_size("pul"), lax.axis_size("sub")
    blocks = puls * subs
    rows = range_len // blocks
    half = rows // 2
    pulse_len = pulse_dev * puls
    size = math.isqrt(pulse_len)
    sub_index = lax.axis_index("sub")
    middle = range_middle(range_phase, math.isqrt(range_len))
    echo = raw_echo.reshape(2, range_len, pulse_dev)
    width = pulse_dev // CHUNKS

    def spread(sent):
        got = lax.all_to_all(sent, ("pul", "sub"), 0, 0, tiled=True)
        return got.reshape(puls, subs, 2, sent.shape[2], width)

    (sent,) = range_compress(echo, middle, 0, width, blocks, 1)
    sent, echo = lax.optimization_barrier((sent, echo))
    every = spread(sent)
    sent_low, sent_high = range_compress(echo, middle, 1, width, blocks, 2)
    own_shift = lax.dynamic_slice_in_dim(migration, sub_index, 1, 0)
    shift = own_shift.reshape(size, size).T
    phase = jnp.swapaxes(doppler.reshape(subs, size, size), 1, 2) * (0.5 / math.pi)
    own_kappa = lax.dynamic_slice_in_dim(kappa, sub_index * rows, rows, 0)
    factors = azimuth_factors(own_kappa, phase)
    every, sent_low, factors = lax.optimization_barrier((every, sent_low, factors))
    got_low = spread(sent_low)
    got_low, sent_high = lax.optimization_barrier((got_low, sent_high))
    low = doppler_forward([every, got_low], [0, 0], half, size)
    place = lambda block: (block % subs) * puls + block // subs
    pairs = [(place(block), place(block - 1)) for block in range(1, blocks)]
    rim = lax.ppermute(low[:, :MAXS], ("sub", "pul"), pairs)
    high = doppler_forward([every, spread(sent_high)], [1, 0], half, size)
    upper = lax.all_to_all(
        image_rows(low, high, factors, 0, shift, subs), "sub", 0, 0, tiled=True
    )
    lower = lax.all_to_all(
        image_rows(high, rim, factors, 1, shift, subs), "sub", 0, 0, tiled=True
    )
    image = jnp.stack([upper, lower], axis=2)
    return jnp.swapaxes(image, 0, 1).reshape(2, rows * subs, pulse_len // subs)


def solution(mesh):
    placed = (P(None, "sub", None, "pul"), P(), P("pul"), P(), P("pul", None))
    return jax.shard_map(
        on_device, mesh=mesh, in_specs=placed, out_specs=P(None, "pul", "sub"), check_vma=False
    )
```

```python
import functools
import math

import jax
import jax.numpy as jnp
import numpy as np
from jax import lax
from jax.experimental import pallas as pl
from jax.experimental.pallas import tpu as pltpu
from jax.sharding import PartitionSpec as P

MAXS = 8
RBLK = 32
LANES = 128
UNROLL = 4
VMEM = 56 * 1024 * 1024
F32 = jnp.float32
BF16 = jnp.bfloat16


def realified(table):
    return np.block([[table.real, -table.imag], [table.imag, table.real]])


def unit_table(rows, cols, length, direction):
    product = np.outer(np.asarray(rows), np.asarray(cols)) % length
    return np.exp(direction * 2j * np.pi * product / length)


def as_bf16(table):
    return np.asarray(table, np.float32).astype(BF16)


def middle_kernel(phase_ref, wave_ref, o_ref):
    cosine, sine = turns(phase_ref[...])
    size = phase_ref.shape[1] // 2
    lane = lax.broadcasted_iota(jnp.int32, sine.shape, 1)
    sine = jnp.where(lane < size, sine, -sine)
    for k2 in range(o_ref.shape[0]):
        wave = wave_ref[k2].astype(F32)
        left = wave * cosine[k2 : k2 + 1] + pltpu.roll(wave, size, 1) * sine[k2 : k2 + 1]
        o_ref[k2] = lax.dot_general(
            left.astype(BF16),
            wave_ref[k2],
            (((1,), (1,)), ((), ())),
            preferred_element_type=F32,
        ).astype(BF16)


def range_middle(range_phase, size):
    length = size * size
    k2 = np.arange(size)[:, None, None]
    j1 = np.arange(size)[None, :, None]
    k1 = np.arange(size)[None, None, :]
    wave = np.exp(2j * np.pi * ((j1 * (k2 + size * k1)) % length) / length) / size
    wave = as_bf16(np.stack([realified(wave[k]) for k in range(size)]))
    phase = range_phase.reshape(size, size).T * (0.5 / math.pi)
    group = 16
    block = pl.BlockSpec((group, 2 * size, 2 * size), lambda i: (i, 0, 0))
    return pl.pallas_call(
        middle_kernel,
        grid=(size // group,),
        in_specs=[pl.BlockSpec((group, 2 * size), lambda i: (i, 0)), block],
        out_specs=block,
        out_shape=jax.ShapeDtypeStruct(wave.shape, BF16),
        compiler_params=pltpu.CompilerParams(vmem_limit_bytes=VMEM),
        name="range_middle",
    )(jnp.concatenate([phase, phase], axis=1), wave)


def range_kernel(size, splits, x_ref, w_ref, t_ref, v_ref, *refs):
    outs, (one, two) = refs[:splits], refs[splits:]
    both = 2 * size
    pitch = size + 1

    def cast(step, carry):
        for u in range(8):
            line = step * 8 + u
            for c in range(2):
                one[pl.ds((c * size + line) * pitch, size), :] = x_ref[
                    c, pl.ds(pl.multiple_of(line * size, size), size), :
                ].astype(F32)
        return carry

    lax.fori_loop(0, size // 8, cast, 0)

    def strided(source, target, table):
        def body(step, carry):
            for u in range(UNROLL):
                j1 = (step * UNROLL + u) * 2
                value = jnp.concatenate(
                    [source[pl.ds(j1 + i, both, stride=pitch), :] for i in range(2)], axis=1
                ).astype(BF16)
                out = jnp.dot(table, value, preferred_element_type=F32)
                for i in range(2):
                    target[pl.ds(j1 + i, both, stride=pitch), :] = out[
                        :, i * LANES : (i + 1) * LANES
                    ]
            return carry

        lax.fori_loop(0, size // (2 * UNROLL), body, 0)

    strided(one, two, w_ref[...])

    def inner(step, carry):
        for u in range(2 * UNROLL):
            k2 = step * 2 * UNROLL + u
            value = jnp.concatenate(
                [two[pl.ds((c * size + k2) * pitch, size), :] for c in range(2)], axis=0
            ).astype(BF16)
            out = jnp.dot(t_ref[k2], value, preferred_element_type=F32)
            for d in range(2):
                one[pl.ds((d * size + k2) * pitch, size), :] = out[d * size : (d + 1) * size]
        return carry

    lax.fori_loop(0, size // (2 * UNROLL), inner, 0)
    strided(one, two, v_ref[...])
    rows = outs[0].shape[2]
    pieces = size // rows

    def give(step, carry):
        for u in range(8):
            line = step * 8 + u
            for piece in range(pieces):
                block = line * (pieces // splits) + piece // splits
                for d in range(2):
                    outs[piece % splits][block, d] = two[
                        pl.ds((d * size + line) * pitch + piece * rows, rows), :
                    ].astype(BF16)
        return carry

    lax.fori_loop(0, size // 8, give, 0)


def range_compress(echo, middle, first, count, blocks, splits):
    length = echo.shape[1]
    size = math.isqrt(length)
    index = np.arange(size)
    forward = as_bf16(realified(unit_table(index, index, size, -1)))
    backward = as_bf16(realified(unit_table(index, index, size, 1)))
    rows = length // blocks // splits
    whole = lambda *shape: pl.BlockSpec(shape, lambda i: (0,) * len(shape))
    scratch = pltpu.VMEM((2 * (length + size), LANES), F32)
    return pl.pallas_call(
        functools.partial(range_kernel, size, splits),
        grid=(count,),
        in_specs=[
            pl.BlockSpec((2, length, LANES), lambda i: (0, 0, first + i)),
            whole(2 * size, 2 * size),
            whole(size, 2 * size, 2 * size),
            whole(2 * size, 2 * size),
        ],
        out_specs=[pl.BlockSpec((blocks, 2, rows, LANES), lambda i: (0, 0, 0, i))] * splits,
        out_shape=[jax.ShapeDtypeStruct((blocks, 2, rows, count * LANES), BF16)] * splits,
        scratch_shapes=[scratch, scratch],
        compiler_params=pltpu.CompilerParams(vmem_limit_bytes=VMEM),
        name="range_compress",
    )(echo, forward, middle, backward)


def doppler_kernel(rows, first, rest, w_ref, cos_ref, sin_ref, u_ref, o_ref, *refs):
    held = refs[-1]
    sources = first.shape[0]
    size = cos_ref.shape[0]
    lines = size // sources
    pitch = rows + 1

    def cast(source, carry):
        for line in range(lines):
            for c in range(2):
                if line == 0:
                    value = first[source, 0, c]
                else:
                    value = rest[source, 0, c, :, (line - 1) * LANES : line * LANES]
                base = (c * lines + line) * sources
                held[pl.ds((base + source) * pitch, rows), :] = value.astype(F32)
        return carry

    lax.fori_loop(0, sources, cast, 0)

    def pair(first_row):
        value = jnp.concatenate(
            [held[pl.ds(first_row + i, 2 * size, stride=pitch), :] for i in range(2)], axis=1
        ).astype(BF16)
        first = jnp.dot(w_ref[...], value, preferred_element_type=F32)
        stacked = []
        for i in range(2):
            real = first[:size, i * LANES : (i + 1) * LANES]
            imag = first[size:, i * LANES : (i + 1) * LANES]
            stacked.append(
                jnp.concatenate(
                    [
                        real * cos_ref[...] - imag * sin_ref[...],
                        real * sin_ref[...] + imag * cos_ref[...],
                    ],
                    axis=1,
                ).astype(BF16)
            )
        second = jnp.dot(
            jnp.concatenate(stacked, axis=0), u_ref[...], preferred_element_type=F32
        ).astype(BF16)
        for i in range(2):
            for d in range(2):
                value = second[i * size : (i + 1) * size, d * LANES : (d + 1) * LANES]
                o_ref[0, first_row + i, d] = value

    def body(step, carry):
        for u in range(4):
            pair(step * 8 + 2 * u)
        return carry

    lax.fori_loop(0, rows // 8, body, 0)
    for rim in refs[:-1]:
        rim[0] = o_ref[0, :MAXS]


def doppler_tables(size, direction):
    index = np.arange(size)
    table = unit_table(index, index, size, direction)
    turn = unit_table(index, index, size * size, direction) / size
    return table, turn.real.astype(np.float32), turn.imag.astype(np.float32)


def doppler_forward(first, rest, part, rows, size, with_rim):
    sources, subs, _, _, width = rest.shape
    table, turn_cos, turn_sin = doppler_tables(size, -1)
    lines = size // sources
    order = np.asarray(
        [lines * source + line for line in range(lines) for source in range(sources)]
    )
    outer = as_bf16(realified(table[:, order]))
    inner = as_bf16(realified(table).T)
    whole = lambda *shape: pl.BlockSpec(shape, lambda i: (0,) * len(shape))
    heights = [rows, MAXS] if with_rim else [rows]
    return pl.pallas_call(
        functools.partial(doppler_kernel, rows),
        grid=(subs,),
        in_specs=[
            pl.BlockSpec((sources, 1, 2, rows, LANES), lambda i: (0, i, 0, part, 0)),
            pl.BlockSpec((sources, 1, 2, rows, width), lambda i: (0, i, 0, 0, 0)),
            whole(2 * size, 2 * size),
            whole(size, size),
            whole(size, size),
            whole(2 * size, 2 * size),
        ],
        out_specs=[
            pl.BlockSpec((1, height, 2, size, size), lambda i: (i, 0, 0, 0, 0))
            for height in heights
        ],
        out_shape=[jax.ShapeDtypeStruct((subs, height, 2, size, size), BF16) for height in heights],
        scratch_shapes=[pltpu.VMEM((2 * size * (rows + 1), LANES), F32)],
        compiler_params=pltpu.CompilerParams(vmem_limit_bytes=VMEM),
        name="doppler_forward",
    )(first, rest, outer, turn_cos, turn_sin, inner)


def turn_polynomials():
    nodes = 0.25 * (1 - np.cos((np.arange(64) + 0.5) * np.pi / 64)) / 2
    roots = np.sqrt(nodes)
    sine = np.polynomial.polynomial.polyfit(nodes, np.sin(2 * np.pi * roots) / roots, 6)
    cosine = np.polynomial.polynomial.polyfit(nodes, np.cos(2 * np.pi * roots), 6)
    return [round(float(v), 7) for v in sine], [round(float(v), 7) for v in cosine]


def turns(cycles):
    sine_terms, cosine_terms = turn_polynomials()
    part = cycles - jnp.floor(cycles + 0.5)
    square = part * part
    sine = jnp.full_like(square, sine_terms[-1])
    cosine = jnp.full_like(square, cosine_terms[-1])
    for term in reversed(sine_terms[:-1]):
        sine = sine * square + term
    for term in reversed(cosine_terms[:-1]):
        cosine = cosine * square + term
    return cosine, sine * part


def factor_kernel(kappa_ref, phase_ref, o_ref):
    def body(step, carry):
        for u in range(2):
            row = step * 2 + u
            cosine, sine = turns(kappa_ref[row] * phase_ref[0])
            o_ref[0, row, 0] = cosine.astype(BF16)
            o_ref[0, row, 1] = sine.astype(BF16)
        return carry

    lax.fori_loop(0, o_ref.shape[1] // 2, body, 0)


def azimuth_factors(kappa, phase):
    subs, size, _ = phase.shape
    rows = kappa.shape[0]
    return pl.pallas_call(
        factor_kernel,
        grid=(subs,),
        in_specs=[
            pl.BlockSpec(memory_space=pltpu.SMEM),
            pl.BlockSpec((1, size, size), lambda i: (i, 0, 0)),
        ],
        out_specs=pl.BlockSpec((1, rows, 2, size, size), lambda i: (i, 0, 0, 0, 0)),
        out_shape=jax.ShapeDtypeStruct((subs, rows, 2, size, size), BF16),
        compiler_params=pltpu.CompilerParams(vmem_limit_bytes=VMEM),
        name="azimuth_factors",
    )(kappa, phase)


def image_kernel(earlier, finish, *refs):
    own, rim, factor_ref, shift_ref, cos_ref, sin_ref, u_ref = refs[:7]
    refs = refs[7:]
    if finish:
        mine_ref, w_ref = refs[:2]
        before, refs = refs[2 : 2 + earlier], refs[2 + earlier :]
        outs, (moved, summed, middle, turned) = refs[:-4], refs[-4:]
    else:
        (out, moved, summed) = refs
    step = pl.program_id(0)
    subs, rows, _, tile, size = own.shape
    shift = shift_ref[...]
    bits = [((shift >> k) & 1).astype(F32).astype(BF16) > 0.5 for k in range(4)]

    def aperture(index, carry):
        for d in range(2):
            values = [own[index, r, d] for r in range(rows)]
            values += [rim[index, r, d] for r in range(MAXS)]
            four = [jnp.where(bits[2], values[r + 4], values[r]) for r in range(rows + 3)]
            two = [jnp.where(bits[1], four[r + 2], four[r]) for r in range(rows + 1)]
            one = [jnp.where(bits[0], two[r + 1], two[r]) for r in range(rows)]
            for r in range(rows):
                moved[index, d, r] = jnp.where(bits[3], values[r + 8], one[r])
        return carry

    lax.fori_loop(0, subs, aperture, 0)

    def row_sum(turn, carry):
        for u in range(4):
            row = turn * 4 + u
            real = jnp.zeros((tile, size), F32)
            imag = jnp.zeros((tile, size), F32)
            for index in range(subs):
                cosine = factor_ref[index, row, 0].astype(F32)
                sine = factor_ref[index, row, 1].astype(F32)
                a, b = moved[index, 0, row].astype(F32), moved[index, 1, row].astype(F32)
                real = real + (a * cosine - b * sine)
                imag = imag + (a * sine + b * cosine)
            summed[pl.ds(pl.multiple_of(row * tile, tile), tile), :] = jnp.concatenate(
                [real, imag], axis=1
            ).astype(BF16)
        return carry

    lax.fori_loop(0, rows // 4, row_sum, 0)
    first = jnp.dot(summed[...], u_ref[...], preferred_element_type=F32)
    for r in range(rows):
        real = first[r * tile : (r + 1) * tile, :size]
        imag = first[r * tile : (r + 1) * tile, size:]
        real, imag = (
            (real * cos_ref[...] - imag * sin_ref[...]).astype(BF16),
            (real * sin_ref[...] + imag * cos_ref[...]).astype(BF16),
        )
        if finish:
            where = pl.ds(pl.multiple_of(step * tile, tile), tile)
            middle[r, 0, where, :] = real
            middle[r, 1, where, :] = imag
        else:
            out[r, 0] = real
            out[r, 1] = imag

    if not finish:
        return

    @pl.when(step == pl.num_programs(0) - 1)
    def _():
        held = [(ref, r) for ref in list(before) + [middle] for r in range(ref.shape[0])]
        pitch = len(held) + 1
        for at in range(0, len(held), 2):
            value = jnp.concatenate(
                [
                    jnp.concatenate([ref[r, c] for c in range(2)], axis=0)
                    for ref, r in held[at : at + 2]
                ],
                axis=1,
            )
            result = jnp.dot(w_ref[...], value, preferred_element_type=F32)
            for i in range(2):
                turned[pl.ds(at + i, 2 * size, stride=pitch), :] = result[
                    :, i * LANES : (i + 1) * LANES
                ]
        per_group = size // len(outs)
        for k, piece in enumerate(outs):
            group = mine_ref[0] ^ k
            for d in range(2):
                for j in range(per_group):
                    line = (d * size + group * per_group + j) * pitch
                    piece[d, :, j * LANES : (j + 1) * LANES] = turned[
                        pl.ds(line, len(held)), :
                    ].astype(BF16)


def image_rows(own, own_at, rows, rim, rim_at, factors, part, shift, mine, groups, before):
    subs, _, _, size, _ = own.shape
    tile = 16
    finish = mine is not None
    table, turn_cos, turn_sin = doppler_tables(size, 1)
    outer = as_bf16(realified(table))
    inner = as_bf16(realified(table).T)
    whole = lambda *shape: pl.BlockSpec(shape, lambda i: (0,) * len(shape))
    lines = pl.BlockSpec((tile, size), lambda i: (i, 0))
    width = size * size // groups
    in_specs = [
        pl.BlockSpec((subs, rows, 2, tile, size), lambda i: (0, own_at, 0, i, 0)),
        pl.BlockSpec((subs, MAXS, 2, tile, size), lambda i: (0, rim_at, 0, i, 0)),
        pl.BlockSpec((subs, rows, 2, tile, size), lambda i: (0, part, 0, i, 0)),
        lines,
        lines,
        lines,
        whole(2 * size, 2 * size),
    ]
    operands = [own, rim, factors, shift, turn_cos, turn_sin, inner]
    scratch = [
        pltpu.VMEM((subs, 2, rows, tile, size), BF16),
        pltpu.VMEM((rows * tile, 2 * size), BF16),
    ]
    if finish:
        total = rows + sum(piece.shape[0] for piece in before)
        in_specs += [pl.BlockSpec(memory_space=pltpu.SMEM), whole(2 * size, 2 * size)]
        in_specs += [whole(*piece.shape) for piece in before]
        operands += [mine, outer, *before]
        out_specs = [whole(2, total, width)] * groups
        out_shape = [jax.ShapeDtypeStruct((2, total, width), BF16)] * groups
        scratch += [
            pltpu.VMEM((rows, 2, size, size), BF16),
            pltpu.VMEM((2 * size * (total + 1), LANES), F32),
        ]
    else:
        out_specs = pl.BlockSpec((rows, 2, tile, size), lambda i: (0, 0, i, 0))
        out_shape = jax.ShapeDtypeStruct((rows, 2, size, size), BF16)
    return pl.pallas_call(
        functools.partial(image_kernel, len(before), finish),
        grid=(size // tile,),
        in_specs=in_specs,
        out_specs=out_specs,
        out_shape=out_shape,
        scratch_shapes=scratch,
        compiler_params=pltpu.CompilerParams(vmem_limit_bytes=VMEM),
        name="image_rows",
    )(*operands)


def place_kernel(mine_ref, *refs):
    pieces, o_ref = refs[:-1], refs[-1]
    rows = pieces[0].shape[1]
    groups = len(pieces) // 2
    for half in range(2):
        for k in range(groups):
            line = (mine_ref[0] ^ k) * 2 * rows + half * rows
            o_ref[0, pl.ds(pl.multiple_of(line, rows), rows), :] = pieces[half * groups + k][0]


def place_rows(mine, pieces):
    _, rows, width = pieces[0].shape
    return pl.pallas_call(
        place_kernel,
        grid=(2,),
        in_specs=[pl.BlockSpec(memory_space=pltpu.SMEM)]
        + [pl.BlockSpec((1, rows, width), lambda i: (i, 0, 0))] * len(pieces),
        out_specs=pl.BlockSpec((1, rows * len(pieces), width), lambda i: (i, 0, 0)),
        out_shape=jax.ShapeDtypeStruct((2, rows * len(pieces), width), BF16),
        compiler_params=pltpu.CompilerParams(vmem_limit_bytes=VMEM),
        name="place_rows",
    )(mine, *pieces)


def on_device(raw_echo, range_phase, kappa, doppler, migration):
    _, _, range_len, pulse_dev = raw_echo.shape
    puls, subs = lax.axis_size("pul"), lax.axis_size("sub")
    blocks = puls * subs
    rows = range_len // blocks
    half = rows // 2
    pulse_len = pulse_dev * puls
    size = math.isqrt(pulse_len)
    sub_index = lax.axis_index("sub")
    mine = sub_index.reshape(1).astype(jnp.int32)
    middle = range_middle(range_phase, math.isqrt(range_len))
    echo = raw_echo.reshape(2, range_len, pulse_dev)

    def spread(sent):
        got = lax.all_to_all(sent, ("pul", "sub"), 0, 0, tiled=True)
        return got.reshape((puls, subs) + sent.shape[1:])

    def swap(pieces):
        sent = [
            lax.ppermute(pieces[k], "sub", [(i, i ^ k) for i in range(subs)])
            for k in range(subs - 1, 0, -1)
        ]
        return [pieces[0]] + sent[::-1]

    (sent,) = range_compress(echo, middle, 0, 1, blocks, 1)
    sent, echo = lax.optimization_barrier((sent, echo))
    first = spread(sent)
    count = pulse_dev // LANES - 1
    sent_low, sent_high = range_compress(echo, middle, 1, count, blocks, 2)
    own_shift = lax.dynamic_slice_in_dim(migration, sub_index, 1, 0)
    shift = own_shift.reshape(size, size).T
    phase = jnp.swapaxes(doppler.reshape(subs, size, size), 1, 2) * (0.5 / math.pi)
    own_kappa = lax.dynamic_slice_in_dim(kappa, sub_index * rows, rows, 0)
    factors = azimuth_factors(own_kappa, phase)
    first, sent_low, factors, shift = lax.optimization_barrier((first, sent_low, factors, shift))
    got_low = spread(sent_low)
    got_low, sent_high = lax.optimization_barrier((got_low, sent_high))
    got_high = spread(sent_high)
    low, edge = doppler_forward(first, got_low, 0, half, size, True)
    place = lambda block: (block % subs) * puls + block // subs
    pairs = [(place(block), place(block - 1)) for block in range(1, blocks)]
    rim = lax.ppermute(edge, ("sub", "pul"), pairs)
    top = image_rows(low, 0, MAXS, low, 1, factors, 0, shift, None, subs, [])
    got_high, top = lax.optimization_barrier((got_high, top))
    (high,) = doppler_forward(first, got_high, 1, half, size, False)
    pieces = image_rows(low, 1, MAXS, high, 0, factors, 1, shift, mine, subs, [top])
    upper = swap(pieces)
    pieces = image_rows(high, 0, half, rim, 0, factors, 1, shift, mine, subs, [])
    lower = swap(pieces)
    return place_rows(mine, upper + lower)


def solution(mesh):
    placed = (P(None, "sub", None, "pul"), P(), P("pul"), P(), P("pul", None))
    return jax.shard_map(
        on_device, mesh=mesh, in_specs=placed, out_specs=P(None, "pul", "sub"), check_vma=False
    )
```

```python
import functools
import math

import jax
import jax.numpy as jnp
import numpy as np
from jax import lax
from jax.experimental import pallas as pl
from jax.experimental.pallas import tpu as pltpu
from jax.sharding import PartitionSpec as P

MAXS = 8
RBLK = 32
LANES = 128
UNROLL = 4
TILE = 32
VMEM = 56 * 1024 * 1024
F32 = jnp.float32
BF16 = jnp.bfloat16


def realified(table):
    return np.block([[table.real, -table.imag], [table.imag, table.real]])


def unit_table(rows, cols, length, direction):
    product = np.outer(np.asarray(rows), np.asarray(cols)) % length
    return np.exp(direction * 2j * np.pi * product / length)


def as_bf16(table):
    return np.asarray(table, np.float32).astype(BF16)


def middle_kernel(phase_ref, wave_ref, o_ref):
    cosine, sine = turns(phase_ref[...])
    size = phase_ref.shape[1] // 2
    lane = lax.broadcasted_iota(jnp.int32, sine.shape, 1)
    sine = jnp.where(lane < size, sine, -sine)
    for k2 in range(o_ref.shape[0]):
        wave = wave_ref[k2].astype(F32)
        left = wave * cosine[k2 : k2 + 1] + pltpu.roll(wave, size, 1) * sine[k2 : k2 + 1]
        o_ref[k2] = lax.dot_general(
            left.astype(BF16),
            wave_ref[k2],
            (((1,), (1,)), ((), ())),
            preferred_element_type=F32,
        ).astype(BF16)


def range_middle(range_phase, size):
    length = size * size
    k2 = np.arange(size)[:, None, None]
    j1 = np.arange(size)[None, :, None]
    k1 = np.arange(size)[None, None, :]
    wave = np.exp(2j * np.pi * ((j1 * (k2 + size * k1)) % length) / length) / size
    wave = as_bf16(np.stack([realified(wave[k]) for k in range(size)]))
    phase = range_phase.reshape(size, size).T * (0.5 / math.pi)
    group = 16
    block = pl.BlockSpec((group, 2 * size, 2 * size), lambda i: (i, 0, 0))
    return pl.pallas_call(
        middle_kernel,
        grid=(size // group,),
        in_specs=[pl.BlockSpec((group, 2 * size), lambda i: (i, 0)), block],
        out_specs=block,
        out_shape=jax.ShapeDtypeStruct(wave.shape, BF16),
        compiler_params=pltpu.CompilerParams(vmem_limit_bytes=VMEM),
        name="range_middle",
    )(jnp.concatenate([phase, phase], axis=1), wave)


def range_kernel(size, splits, x_ref, w_ref, t_ref, v_ref, *refs):
    outs, (one, two) = refs[:splits], refs[splits:]
    both = 2 * size
    pitch = size + 1

    def cast(step, carry):
        for u in range(8):
            line = step * 8 + u
            for c in range(2):
                one[pl.ds((c * size + line) * pitch, size), :] = x_ref[
                    c, pl.ds(pl.multiple_of(line * size, size), size), :
                ].astype(F32)
        return carry

    lax.fori_loop(0, size // 8, cast, 0)

    def strided(source, target, table):
        def body(step, carry):
            for u in range(UNROLL):
                j1 = (step * UNROLL + u) * 2
                value = jnp.concatenate(
                    [source[pl.ds(j1 + i, both, stride=pitch), :] for i in range(2)], axis=1
                ).astype(BF16)
                out = jnp.dot(table, value, preferred_element_type=F32)
                for i in range(2):
                    target[pl.ds(j1 + i, both, stride=pitch), :] = out[
                        :, i * LANES : (i + 1) * LANES
                    ]
            return carry

        lax.fori_loop(0, size // (2 * UNROLL), body, 0)

    strided(one, two, w_ref[...])

    def inner(step, carry):
        for u in range(2 * UNROLL):
            k2 = step * 2 * UNROLL + u
            value = jnp.concatenate(
                [two[pl.ds((c * size + k2) * pitch, size), :] for c in range(2)], axis=0
            ).astype(BF16)
            out = jnp.dot(t_ref[k2], value, preferred_element_type=F32)
            for d in range(2):
                one[pl.ds((d * size + k2) * pitch, size), :] = out[d * size : (d + 1) * size]
        return carry

    lax.fori_loop(0, size // (2 * UNROLL), inner, 0)
    strided(one, two, v_ref[...])
    rows = outs[0].shape[2]
    pieces = size // rows

    def give(step, carry):
        for u in range(8):
            line = step * 8 + u
            for piece in range(pieces):
                block = line * (pieces // splits) + piece // splits
                for d in range(2):
                    outs[piece % splits][block, d] = two[
                        pl.ds((d * size + line) * pitch + piece * rows, rows), :
                    ].astype(BF16)
        return carry

    lax.fori_loop(0, size // 8, give, 0)


def range_compress(echo, middle, first, count, blocks, splits):
    length = echo.shape[1]
    size = math.isqrt(length)
    index = np.arange(size)
    forward = as_bf16(realified(unit_table(index, index, size, -1)))
    backward = as_bf16(realified(unit_table(index, index, size, 1)))
    rows = length // blocks // splits
    whole = lambda *shape: pl.BlockSpec(shape, lambda i: (0,) * len(shape))
    scratch = pltpu.VMEM((2 * (length + size), LANES), F32)
    return pl.pallas_call(
        functools.partial(range_kernel, size, splits),
        grid=(count,),
        in_specs=[
            pl.BlockSpec((2, length, LANES), lambda i: (0, 0, first + i)),
            whole(2 * size, 2 * size),
            whole(size, 2 * size, 2 * size),
            whole(2 * size, 2 * size),
        ],
        out_specs=[pl.BlockSpec((blocks, 2, rows, LANES), lambda i: (0, 0, 0, i))] * splits,
        out_shape=[jax.ShapeDtypeStruct((blocks, 2, rows, count * LANES), BF16)] * splits,
        scratch_shapes=[scratch, scratch],
        compiler_params=pltpu.CompilerParams(vmem_limit_bytes=VMEM),
        name="range_compress",
    )(echo, forward, middle, backward)


def doppler_kernel(rows, first, rest, w_ref, cos_ref, sin_ref, u_ref, o_ref, *refs):
    held = refs[-1]
    sources = first.shape[0]
    size = cos_ref.shape[0]
    lines = size // sources
    pitch = rows + 1

    def cast(source, carry):
        for line in range(lines):
            for c in range(2):
                if line == 0:
                    value = first[source, 0, c]
                else:
                    value = rest[source, 0, c, :, (line - 1) * LANES : line * LANES]
                base = (c * lines + line) * sources
                held[pl.ds((base + source) * pitch, rows), :] = value.astype(F32)
        return carry

    lax.fori_loop(0, sources, cast, 0)

    def pair(first_row):
        value = jnp.concatenate(
            [held[pl.ds(first_row + i, 2 * size, stride=pitch), :] for i in range(2)], axis=1
        ).astype(BF16)
        first = jnp.dot(w_ref[...], value, preferred_element_type=F32)
        stacked = []
        for i in range(2):
            real = first[:size, i * LANES : (i + 1) * LANES]
            imag = first[size:, i * LANES : (i + 1) * LANES]
            stacked.append(
                jnp.concatenate(
                    [
                        real * cos_ref[...] - imag * sin_ref[...],
                        real * sin_ref[...] + imag * cos_ref[...],
                    ],
                    axis=1,
                ).astype(BF16)
            )
        second = jnp.dot(
            jnp.concatenate(stacked, axis=0), u_ref[...], preferred_element_type=F32
        ).astype(BF16)
        for i in range(2):
            for d in range(2):
                for tile in range(size // TILE):
                    line = i * size + tile * TILE
                    value = second[line : line + TILE, d * LANES : (d + 1) * LANES]
                    o_ref[tile, 0, first_row + i, d] = value

    def body(step, carry):
        for u in range(4):
            pair(step * 8 + 2 * u)
        return carry

    lax.fori_loop(0, rows // 8, body, 0)
    for rim in refs[:-1]:
        rim[:, 0] = o_ref[:, 0, :MAXS]


def doppler_tables(size, direction):
    index = np.arange(size)
    table = unit_table(index, index, size, direction)
    turn = unit_table(index, index, size * size, direction) / size
    return table, turn.real.astype(np.float32), turn.imag.astype(np.float32)


def doppler_forward(first, rest, part, rows, size, with_rim):
    sources, subs, _, _, width = rest.shape
    table, turn_cos, turn_sin = doppler_tables(size, -1)
    lines = size // sources
    order = np.asarray(
        [lines * source + line for line in range(lines) for source in range(sources)]
    )
    outer = as_bf16(realified(table[:, order]))
    inner = as_bf16(realified(table).T)
    whole = lambda *shape: pl.BlockSpec(shape, lambda i: (0,) * len(shape))
    heights = [rows, MAXS] if with_rim else [rows]
    return pl.pallas_call(
        functools.partial(doppler_kernel, rows),
        grid=(subs,),
        in_specs=[
            pl.BlockSpec((sources, 1, 2, rows, LANES), lambda i: (0, i, 0, part, 0)),
            pl.BlockSpec((sources, 1, 2, rows, width), lambda i: (0, i, 0, 0, 0)),
            whole(2 * size, 2 * size),
            whole(size, size),
            whole(size, size),
            whole(2 * size, 2 * size),
        ],
        out_specs=[
            pl.BlockSpec((size // TILE, 1, height, 2, TILE, size), lambda i: (0, i, 0, 0, 0, 0))
            for height in heights
        ],
        out_shape=[
            jax.ShapeDtypeStruct((size // TILE, subs, height, 2, TILE, size), BF16)
            for height in heights
        ],
        scratch_shapes=[pltpu.VMEM((2 * size * (rows + 1), LANES), F32)],
        compiler_params=pltpu.CompilerParams(vmem_limit_bytes=VMEM),
        name="doppler_forward",
    )(first, rest, outer, turn_cos, turn_sin, inner)


def turn_polynomials():
    nodes = 0.25 * (1 - np.cos((np.arange(64) + 0.5) * np.pi / 64)) / 2
    roots = np.sqrt(nodes)
    sine = np.polynomial.polynomial.polyfit(nodes, np.sin(2 * np.pi * roots) / roots, 6)
    cosine = np.polynomial.polynomial.polyfit(nodes, np.cos(2 * np.pi * roots), 6)
    return [round(float(v), 7) for v in sine], [round(float(v), 7) for v in cosine]


def turns(cycles):
    sine_terms, cosine_terms = turn_polynomials()
    part = cycles - jnp.floor(cycles + 0.5)
    square = part * part
    sine = jnp.full_like(square, sine_terms[-1])
    cosine = jnp.full_like(square, cosine_terms[-1])
    for term in reversed(sine_terms[:-1]):
        sine = sine * square + term
    for term in reversed(cosine_terms[:-1]):
        cosine = cosine * square + term
    return cosine, sine * part


def factor_kernel(kappa_ref, phase_ref, o_ref):
    def body(step, carry):
        for u in range(2):
            row = step * 2 + u
            for tile in range(o_ref.shape[0]):
                cosine, sine = turns(kappa_ref[row] * phase_ref[0, tile * TILE : (tile + 1) * TILE])
                o_ref[tile, 0, row, 0] = cosine.astype(BF16)
                o_ref[tile, 0, row, 1] = sine.astype(BF16)
        return carry

    lax.fori_loop(0, o_ref.shape[2] // 2, body, 0)


def azimuth_factors(kappa, phase):
    subs, size, _ = phase.shape
    rows = kappa.shape[0]
    return pl.pallas_call(
        factor_kernel,
        grid=(subs,),
        in_specs=[
            pl.BlockSpec(memory_space=pltpu.SMEM),
            pl.BlockSpec((1, size, size), lambda i: (i, 0, 0)),
        ],
        out_specs=pl.BlockSpec(
            (size // TILE, 1, rows, 2, TILE, size), lambda i: (0, i, 0, 0, 0, 0)
        ),
        out_shape=jax.ShapeDtypeStruct((size // TILE, subs, rows, 2, TILE, size), BF16),
        compiler_params=pltpu.CompilerParams(vmem_limit_bytes=VMEM),
        name="azimuth_factors",
    )(kappa, phase)


def image_kernel(earlier, finish, *refs):
    own, rim, factor_ref, shift_ref, cos_ref, sin_ref, u_ref = refs[:7]
    refs = refs[7:]
    if finish:
        mine_ref, w_ref = refs[:2]
        before, refs = refs[2 : 2 + earlier], refs[2 + earlier :]
        outs, (moved, summed, middle, turned) = refs[:-4], refs[-4:]
    else:
        (out, moved, summed) = refs
    step = pl.program_id(0)
    _, subs, rows, _, tile, size = own.shape
    shift = shift_ref[...]
    bits = [((shift >> k) & 1).astype(F32).astype(BF16) > 0.5 for k in range(4)]

    def aperture(index, carry):
        for d in range(2):
            values = [own[0, index, r, d] for r in range(rows)]
            values += [rim[0, index, r, d] for r in range(MAXS)]
            four = [jnp.where(bits[2], values[r + 4], values[r]) for r in range(rows + 3)]
            two = [jnp.where(bits[1], four[r + 2], four[r]) for r in range(rows + 1)]
            one = [jnp.where(bits[0], two[r + 1], two[r]) for r in range(rows)]
            for r in range(rows):
                moved[index, d, r] = jnp.where(bits[3], values[r + 8], one[r])
        return carry

    lax.fori_loop(0, subs, aperture, 0)

    def row_sum(turn, carry):
        for u in range(4):
            row = turn * 4 + u
            real = jnp.zeros((tile, size), F32)
            imag = jnp.zeros((tile, size), F32)
            for index in range(subs):
                cosine = factor_ref[0, index, row, 0].astype(F32)
                sine = factor_ref[0, index, row, 1].astype(F32)
                a, b = moved[index, 0, row].astype(F32), moved[index, 1, row].astype(F32)
                real = real + (a * cosine - b * sine)
                imag = imag + (a * sine + b * cosine)
            summed[pl.ds(pl.multiple_of(row * tile, tile), tile), :] = jnp.concatenate(
                [real, imag], axis=1
            ).astype(BF16)
        return carry

    lax.fori_loop(0, rows // 4, row_sum, 0)
    first = jnp.dot(summed[...], u_ref[...], preferred_element_type=F32)
    for r in range(rows):
        real = first[r * tile : (r + 1) * tile, :size]
        imag = first[r * tile : (r + 1) * tile, size:]
        real, imag = (
            (real * cos_ref[...] - imag * sin_ref[...]).astype(BF16),
            (real * sin_ref[...] + imag * cos_ref[...]).astype(BF16),
        )
        if finish:
            where = pl.ds(pl.multiple_of(step * tile, tile), tile)
            middle[r, 0, where, :] = real
            middle[r, 1, where, :] = imag
        else:
            out[r, 0] = real
            out[r, 1] = imag

    if not finish:
        return

    @pl.when(step == pl.num_programs(0) - 1)
    def _():
        held = [(ref, r) for ref in list(before) + [middle] for r in range(ref.shape[0])]
        pitch = len(held) + 1
        for at in range(0, len(held), 2):
            value = jnp.concatenate(
                [
                    jnp.concatenate([ref[r, c] for c in range(2)], axis=0)
                    for ref, r in held[at : at + 2]
                ],
                axis=1,
            )
            result = jnp.dot(w_ref[...], value, preferred_element_type=F32)
            for i in range(2):
                turned[pl.ds(at + i, 2 * size, stride=pitch), :] = result[
                    :, i * LANES : (i + 1) * LANES
                ]
        per_group = size // len(outs)
        for k, piece in enumerate(outs):
            group = mine_ref[0] ^ k
            for d in range(2):
                for j in range(per_group):
                    line = (d * size + group * per_group + j) * pitch
                    piece[d, :, j * LANES : (j + 1) * LANES] = turned[
                        pl.ds(line, len(held)), :
                    ].astype(BF16)


def image_rows(own, own_at, rows, rim, rim_at, factors, part, shift, mine, groups, before):
    _, subs, _, _, tile, size = own.shape
    finish = mine is not None
    table, turn_cos, turn_sin = doppler_tables(size, 1)
    outer = as_bf16(realified(table))
    inner = as_bf16(realified(table).T)
    whole = lambda *shape: pl.BlockSpec(shape, lambda i: (0,) * len(shape))
    lines = pl.BlockSpec((tile, size), lambda i: (i, 0))
    width = size * size // groups
    in_specs = [
        pl.BlockSpec((1, subs, rows, 2, tile, size), lambda i: (i, 0, own_at, 0, 0, 0)),
        pl.BlockSpec((1, subs, MAXS, 2, tile, size), lambda i: (i, 0, rim_at, 0, 0, 0)),
        pl.BlockSpec((1, subs, rows, 2, tile, size), lambda i: (i, 0, part, 0, 0, 0)),
        lines,
        lines,
        lines,
        whole(2 * size, 2 * size),
    ]
    operands = [own, rim, factors, shift, turn_cos, turn_sin, inner]
    scratch = [
        pltpu.VMEM((subs, 2, rows, tile, size), BF16),
        pltpu.VMEM((rows * tile, 2 * size), BF16),
    ]
    if finish:
        total = rows + sum(piece.shape[0] for piece in before)
        in_specs += [pl.BlockSpec(memory_space=pltpu.SMEM), whole(2 * size, 2 * size)]
        in_specs += [whole(*piece.shape) for piece in before]
        operands += [mine, outer, *before]
        out_specs = [whole(2, total, width)] * groups
        out_shape = [jax.ShapeDtypeStruct((2, total, width), BF16)] * groups
        scratch += [
            pltpu.VMEM((rows, 2, size, size), BF16),
            pltpu.VMEM((2 * size * (total + 1), LANES), F32),
        ]
    else:
        out_specs = pl.BlockSpec((rows, 2, tile, size), lambda i: (0, 0, i, 0))
        out_shape = jax.ShapeDtypeStruct((rows, 2, size, size), BF16)
    return pl.pallas_call(
        functools.partial(image_kernel, len(before), finish),
        grid=(size // tile,),
        in_specs=in_specs,
        out_specs=out_specs,
        out_shape=out_shape,
        scratch_shapes=scratch,
        compiler_params=pltpu.CompilerParams(vmem_limit_bytes=VMEM),
        name="image_rows",
    )(*operands)


def place_kernel(mine_ref, *refs):
    pieces, o_ref = refs[:-1], refs[-1]
    rows = pieces[0].shape[1]
    groups = len(pieces) // 2
    for half in range(2):
        for k in range(groups):
            line = (mine_ref[0] ^ k) * 2 * rows + half * rows
            o_ref[0, pl.ds(pl.multiple_of(line, rows), rows), :] = pieces[half * groups + k][0]


def place_rows(mine, pieces):
    _, rows, width = pieces[0].shape
    return pl.pallas_call(
        place_kernel,
        grid=(2,),
        in_specs=[pl.BlockSpec(memory_space=pltpu.SMEM)]
        + [pl.BlockSpec((1, rows, width), lambda i: (i, 0, 0))] * len(pieces),
        out_specs=pl.BlockSpec((1, rows * len(pieces), width), lambda i: (i, 0, 0)),
        out_shape=jax.ShapeDtypeStruct((2, rows * len(pieces), width), BF16),
        compiler_params=pltpu.CompilerParams(vmem_limit_bytes=VMEM),
        name="place_rows",
    )(mine, *pieces)


def on_device(raw_echo, range_phase, kappa, doppler, migration):
    _, _, range_len, pulse_dev = raw_echo.shape
    puls, subs = lax.axis_size("pul"), lax.axis_size("sub")
    blocks = puls * subs
    rows = range_len // blocks
    half = rows // 2
    pulse_len = pulse_dev * puls
    size = math.isqrt(pulse_len)
    sub_index = lax.axis_index("sub")
    mine = sub_index.reshape(1).astype(jnp.int32)
    middle = range_middle(range_phase, math.isqrt(range_len))
    echo = raw_echo.reshape(2, range_len, pulse_dev)

    def spread(sent):
        got = lax.all_to_all(sent, ("pul", "sub"), 0, 0, tiled=True)
        return got.reshape((puls, subs) + sent.shape[1:])

    def swap(pieces):
        sent = [
            lax.ppermute(pieces[k], "sub", [(i, i ^ k) for i in range(subs)])
            for k in range(subs - 1, 0, -1)
        ]
        return [pieces[0]] + sent[::-1]

    (sent,) = range_compress(echo, middle, 0, 1, blocks, 1)
    sent, echo = lax.optimization_barrier((sent, echo))
    first = spread(sent)
    count = pulse_dev // LANES - 1
    sent_low, sent_high = range_compress(echo, middle, 1, count, blocks, 2)
    own_shift = lax.dynamic_slice_in_dim(migration, sub_index, 1, 0)
    shift = own_shift.reshape(size, size).T
    phase = jnp.swapaxes(doppler.reshape(subs, size, size), 1, 2) * (0.5 / math.pi)
    own_kappa = lax.dynamic_slice_in_dim(kappa, sub_index * rows, rows, 0)
    first, sent_low, phase, own_kappa, shift = lax.optimization_barrier(
        (first, sent_low, phase, own_kappa, shift)
    )
    got_low = spread(sent_low)
    got_low, sent_high = lax.optimization_barrier((got_low, sent_high))
    got_high = spread(sent_high)
    low, edge = doppler_forward(first, got_low, 0, half, size, True)
    low, own_kappa = lax.optimization_barrier((low, own_kappa))
    factors = azimuth_factors(own_kappa, phase)
    place = lambda block: (block % subs) * puls + block // subs
    pairs = [(place(block), place(block - 1)) for block in range(1, blocks)]
    top = image_rows(low, 0, MAXS, low, 1, factors, 0, shift, None, subs, [])
    top, edge = lax.optimization_barrier((top, edge))
    rim = lax.ppermute(edge, ("sub", "pul"), pairs)
    got_high, top = lax.optimization_barrier((got_high, top))
    (high,) = doppler_forward(first, got_high, 1, half, size, False)
    pieces = image_rows(low, 1, MAXS, high, 0, factors, 1, shift, mine, subs, [top])
    upper = swap(pieces)
    pieces = image_rows(high, 0, half, rim, 0, factors, 1, shift, mine, subs, [])
    lower = swap(pieces)
    return place_rows(mine, upper + lower)


def solution(mesh):
    placed = (P(None, "sub", None, "pul"), P(), P("pul"), P(), P("pul", None))
    return jax.shard_map(
        on_device, mesh=mesh, in_specs=placed, out_specs=P(None, "pul", "sub"), check_vma=False
    )
```

```python
import functools
import math

import jax
import jax.numpy as jnp
import numpy as np
from jax import lax
from jax.experimental import pallas as pl
from jax.experimental.pallas import tpu as pltpu
from jax.sharding import PartitionSpec as P

MAXS = 8
RBLK = 32
LANES = 128
UNROLL = 4
TILE = 32
VMEM = 56 * 1024 * 1024
F32 = jnp.float32
BF16 = jnp.bfloat16


def realified(table):
    return np.block([[table.real, -table.imag], [table.imag, table.real]])


def unit_table(rows, cols, length, direction):
    product = np.outer(np.asarray(rows), np.asarray(cols)) % length
    return np.exp(direction * 2j * np.pi * product / length)


def as_bf16(table):
    return np.asarray(table, np.float32).astype(BF16)


def middle_kernel(phase_ref, wave_ref, o_ref):
    cosine, sine = turns(phase_ref[...])
    size = phase_ref.shape[1] // 2
    lane = lax.broadcasted_iota(jnp.int32, sine.shape, 1)
    sine = jnp.where(lane < size, sine, -sine)
    for k2 in range(o_ref.shape[0]):
        wave = wave_ref[k2].astype(F32)
        left = wave * cosine[k2 : k2 + 1] + pltpu.roll(wave, size, 1) * sine[k2 : k2 + 1]
        o_ref[k2] = lax.dot_general(
            left.astype(BF16),
            wave_ref[k2],
            (((1,), (1,)), ((), ())),
            preferred_element_type=F32,
        ).astype(BF16)


def range_middle(range_phase, size):
    length = size * size
    k2 = np.arange(size)[:, None, None]
    j1 = np.arange(size)[None, :, None]
    k1 = np.arange(size)[None, None, :]
    wave = np.exp(2j * np.pi * ((j1 * (k2 + size * k1)) % length) / length) / size
    wave = as_bf16(np.stack([realified(wave[k]) for k in range(size)]))
    phase = range_phase.reshape(size, size).T * (0.5 / math.pi)
    group = 16
    block = pl.BlockSpec((group, 2 * size, 2 * size), lambda i: (i, 0, 0))
    return pl.pallas_call(
        middle_kernel,
        grid=(size // group,),
        in_specs=[pl.BlockSpec((group, 2 * size), lambda i: (i, 0)), block],
        out_specs=block,
        out_shape=jax.ShapeDtypeStruct(wave.shape, BF16),
        compiler_params=pltpu.CompilerParams(vmem_limit_bytes=VMEM),
        name="range_middle",
    )(jnp.concatenate([phase, phase], axis=1), wave)


def range_kernel(size, splits, x_ref, w_ref, t_ref, v_ref, *refs):
    outs, (one, two) = refs[:splits], refs[splits:]
    both = 2 * size
    pitch = size + 1

    def cast(step, carry):
        for u in range(8):
            line = step * 8 + u
            for c in range(2):
                one[pl.ds((c * size + line) * pitch, size), :] = x_ref[
                    c, pl.ds(pl.multiple_of(line * size, size), size), :
                ].astype(F32)
        return carry

    lax.fori_loop(0, size // 8, cast, 0)

    def strided(source, target, table):
        def body(step, carry):
            for u in range(UNROLL):
                j1 = (step * UNROLL + u) * 2
                value = jnp.concatenate(
                    [source[pl.ds(j1 + i, both, stride=pitch), :] for i in range(2)], axis=1
                ).astype(BF16)
                out = jnp.dot(table, value, preferred_element_type=F32)
                for i in range(2):
                    target[pl.ds(j1 + i, both, stride=pitch), :] = out[
                        :, i * LANES : (i + 1) * LANES
                    ]
            return carry

        lax.fori_loop(0, size // (2 * UNROLL), body, 0)

    strided(one, two, w_ref[...])

    def inner(step, carry):
        for u in range(2 * UNROLL):
            k2 = step * 2 * UNROLL + u
            value = jnp.concatenate(
                [two[pl.ds((c * size + k2) * pitch, size), :] for c in range(2)], axis=0
            ).astype(BF16)
            out = jnp.dot(t_ref[k2], value, preferred_element_type=F32)
            for d in range(2):
                one[pl.ds((d * size + k2) * pitch, size), :] = out[d * size : (d + 1) * size]
        return carry

    lax.fori_loop(0, size // (2 * UNROLL), inner, 0)
    strided(one, two, v_ref[...])
    rows = outs[0].shape[2]
    pieces = size // rows

    def give(step, carry):
        for u in range(8):
            line = step * 8 + u
            for piece in range(pieces):
                block = line * (pieces // splits) + piece // splits
                for d in range(2):
                    outs[piece % splits][block, d] = two[
                        pl.ds((d * size + line) * pitch + piece * rows, rows), :
                    ].astype(BF16)
        return carry

    lax.fori_loop(0, size // 8, give, 0)


def range_compress(echo, middle, first, count, blocks, splits):
    length = echo.shape[1]
    size = math.isqrt(length)
    index = np.arange(size)
    forward = as_bf16(realified(unit_table(index, index, size, -1)))
    backward = as_bf16(realified(unit_table(index, index, size, 1)))
    rows = length // blocks // splits
    whole = lambda *shape: pl.BlockSpec(shape, lambda i: (0,) * len(shape))
    scratch = pltpu.VMEM((2 * (length + size), LANES), F32)
    return pl.pallas_call(
        functools.partial(range_kernel, size, splits),
        grid=(count,),
        in_specs=[
            pl.BlockSpec((2, length, LANES), lambda i: (0, 0, first + i)),
            whole(2 * size, 2 * size),
            whole(size, 2 * size, 2 * size),
            whole(2 * size, 2 * size),
        ],
        out_specs=[pl.BlockSpec((blocks, 2, rows, LANES), lambda i: (0, 0, 0, i))] * splits,
        out_shape=[jax.ShapeDtypeStruct((blocks, 2, rows, count * LANES), BF16)] * splits,
        scratch_shapes=[scratch, scratch],
        compiler_params=pltpu.CompilerParams(vmem_limit_bytes=VMEM),
        name="range_compress",
    )(echo, forward, middle, backward)


def doppler_kernel(rows, first, rest, w_ref, cos_ref, sin_ref, u_ref, o_ref, *refs):
    held = refs[-1]
    sources = first.shape[0]
    size = cos_ref.shape[0]
    lines = size // sources
    pitch = rows + 1

    def cast(source, carry):
        for line in range(lines):
            for c in range(2):
                if line == 0:
                    value = first[source, 0, c]
                else:
                    value = rest[source, 0, c, :, (line - 1) * LANES : line * LANES]
                base = (c * lines + line) * sources
                held[pl.ds((base + source) * pitch, rows), :] = value.astype(F32)
        return carry

    lax.fori_loop(0, sources, cast, 0)

    def pair(first_row):
        value = jnp.concatenate(
            [held[pl.ds(first_row + i, 2 * size, stride=pitch), :] for i in range(2)], axis=1
        ).astype(BF16)
        first = jnp.dot(w_ref[...], value, preferred_element_type=F32)
        stacked = []
        for i in range(2):
            real = first[:size, i * LANES : (i + 1) * LANES]
            imag = first[size:, i * LANES : (i + 1) * LANES]
            stacked.append(
                jnp.concatenate(
                    [
                        real * cos_ref[...] - imag * sin_ref[...],
                        real * sin_ref[...] + imag * cos_ref[...],
                    ],
                    axis=1,
                ).astype(BF16)
            )
        second = jnp.dot(
            jnp.concatenate(stacked, axis=0), u_ref[...], preferred_element_type=F32
        ).astype(BF16)
        for i in range(2):
            for d in range(2):
                for tile in range(size // TILE):
                    line = i * size + tile * TILE
                    value = second[line : line + TILE, d * LANES : (d + 1) * LANES]
                    o_ref[tile, 0, first_row + i, d] = value

    def body(step, carry):
        for u in range(4):
            pair(step * 8 + 2 * u)
        return carry

    lax.fori_loop(0, rows // 8, body, 0)
    for rim in refs[:-1]:
        rim[:, 0] = o_ref[:, 0, :MAXS]


def doppler_tables(size, direction):
    index = np.arange(size)
    table = unit_table(index, index, size, direction)
    turn = unit_table(index, index, size * size, direction) / size
    return table, turn.real.astype(np.float32), turn.imag.astype(np.float32)


def doppler_forward(first, rest, part, rows, size, with_rim):
    sources, subs, _, _, width = rest.shape
    table, turn_cos, turn_sin = doppler_tables(size, -1)
    lines = size // sources
    order = np.asarray(
        [lines * source + line for line in range(lines) for source in range(sources)]
    )
    outer = as_bf16(realified(table[:, order]))
    inner = as_bf16(realified(table).T)
    whole = lambda *shape: pl.BlockSpec(shape, lambda i: (0,) * len(shape))
    heights = [rows, MAXS] if with_rim else [rows]
    return pl.pallas_call(
        functools.partial(doppler_kernel, rows),
        grid=(subs,),
        in_specs=[
            pl.BlockSpec((sources, 1, 2, rows, LANES), lambda i: (0, i, 0, part, 0)),
            pl.BlockSpec((sources, 1, 2, rows, width), lambda i: (0, i, 0, 0, 0)),
            whole(2 * size, 2 * size),
            whole(size, size),
            whole(size, size),
            whole(2 * size, 2 * size),
        ],
        out_specs=[
            pl.BlockSpec((size // TILE, 1, height, 2, TILE, size), lambda i: (0, i, 0, 0, 0, 0))
            for height in heights
        ],
        out_shape=[
            jax.ShapeDtypeStruct((size // TILE, subs, height, 2, TILE, size), BF16)
            for height in heights
        ],
        scratch_shapes=[pltpu.VMEM((2 * size * (rows + 1), LANES), F32)],
        compiler_params=pltpu.CompilerParams(vmem_limit_bytes=VMEM),
        name="doppler_forward",
    )(first, rest, outer, turn_cos, turn_sin, inner)


def turn_polynomials():
    nodes = 0.25 * (1 - np.cos((np.arange(64) + 0.5) * np.pi / 64)) / 2
    roots = np.sqrt(nodes)
    sine = np.polynomial.polynomial.polyfit(nodes, np.sin(2 * np.pi * roots) / roots, 6)
    cosine = np.polynomial.polynomial.polyfit(nodes, np.cos(2 * np.pi * roots), 6)
    return [round(float(v), 7) for v in sine], [round(float(v), 7) for v in cosine]


def turns(cycles):
    sine_terms, cosine_terms = turn_polynomials()
    part = cycles - jnp.floor(cycles + 0.5)
    square = part * part
    sine = jnp.full_like(square, sine_terms[-1])
    cosine = jnp.full_like(square, cosine_terms[-1])
    for term in reversed(sine_terms[:-1]):
        sine = sine * square + term
    for term in reversed(cosine_terms[:-1]):
        cosine = cosine * square + term
    return cosine, sine * part


def factor_kernel(kappa_ref, phase_ref, o_ref):
    def body(step, carry):
        for u in range(2):
            row = step * 2 + u
            for tile in range(o_ref.shape[0]):
                cosine, sine = turns(kappa_ref[row] * phase_ref[0, tile * TILE : (tile + 1) * TILE])
                o_ref[tile, 0, row, 0] = cosine.astype(BF16)
                o_ref[tile, 0, row, 1] = sine.astype(BF16)
        return carry

    lax.fori_loop(0, o_ref.shape[2] // 2, body, 0)


def azimuth_factors(kappa, phase):
    subs, size, _ = phase.shape
    rows = kappa.shape[0]
    return pl.pallas_call(
        factor_kernel,
        grid=(subs,),
        in_specs=[
            pl.BlockSpec(memory_space=pltpu.SMEM),
            pl.BlockSpec((1, size, size), lambda i: (i, 0, 0)),
        ],
        out_specs=pl.BlockSpec(
            (size // TILE, 1, rows, 2, TILE, size), lambda i: (0, i, 0, 0, 0, 0)
        ),
        out_shape=jax.ShapeDtypeStruct((size // TILE, subs, rows, 2, TILE, size), BF16),
        compiler_params=pltpu.CompilerParams(vmem_limit_bytes=VMEM),
        name="azimuth_factors",
    )(kappa, phase)


def image_kernel(earlier, finish, *refs):
    own, rim, factor_ref, shift_ref, cos_ref, sin_ref, u_ref = refs[:7]
    refs = refs[7:]
    if finish:
        mine_ref, w_ref = refs[:2]
        before, refs = refs[2 : 2 + earlier], refs[2 + earlier :]
        outs, (moved, summed, middle, turned) = refs[:-4], refs[-4:]
    else:
        (out, moved, summed) = refs
    step = pl.program_id(0)
    _, subs, rows, _, tile, size = own.shape
    shift = shift_ref[...]
    bits = [((shift >> k) & 1).astype(F32).astype(BF16) > 0.5 for k in range(4)]

    def aperture(index, carry):
        for d in range(2):
            values = [own[0, index, r, d] for r in range(rows)]
            values += [rim[0, index, r, d] for r in range(MAXS)]
            four = [jnp.where(bits[2], values[r + 4], values[r]) for r in range(rows + 3)]
            two = [jnp.where(bits[1], four[r + 2], four[r]) for r in range(rows + 1)]
            one = [jnp.where(bits[0], two[r + 1], two[r]) for r in range(rows)]
            for r in range(rows):
                moved[index, d, r] = jnp.where(bits[3], values[r + 8], one[r])
        return carry

    lax.fori_loop(0, subs, aperture, 0)

    def row_sum(turn, carry):
        for u in range(4):
            row = turn * 4 + u
            real = jnp.zeros((tile, size), F32)
            imag = jnp.zeros((tile, size), F32)
            for index in range(subs):
                cosine = factor_ref[0, index, row, 0].astype(F32)
                sine = factor_ref[0, index, row, 1].astype(F32)
                a, b = moved[index, 0, row].astype(F32), moved[index, 1, row].astype(F32)
                real = real + (a * cosine - b * sine)
                imag = imag + (a * sine + b * cosine)
            summed[pl.ds(pl.multiple_of(row * tile, tile), tile), :] = jnp.concatenate(
                [real, imag], axis=1
            ).astype(BF16)
        return carry

    lax.fori_loop(0, rows // 4, row_sum, 0)
    first = jnp.dot(summed[...], u_ref[...], preferred_element_type=F32)
    for r in range(rows):
        real = first[r * tile : (r + 1) * tile, :size]
        imag = first[r * tile : (r + 1) * tile, size:]
        real, imag = (
            (real * cos_ref[...] - imag * sin_ref[...]).astype(BF16),
            (real * sin_ref[...] + imag * cos_ref[...]).astype(BF16),
        )
        if finish:
            where = pl.ds(pl.multiple_of(step * tile, tile), tile)
            middle[r, 0, where, :] = real
            middle[r, 1, where, :] = imag
        else:
            out[r, 0] = real
            out[r, 1] = imag

    if not finish:
        return

    @pl.when(step == pl.num_programs(0) - 1)
    def _():
        held = [(ref, r) for ref in list(before) + [middle] for r in range(ref.shape[0])]
        pitch = len(held) + 1
        for at in range(0, len(held), 2):
            value = jnp.concatenate(
                [
                    jnp.concatenate([ref[r, c] for c in range(2)], axis=0)
                    for ref, r in held[at : at + 2]
                ],
                axis=1,
            )
            result = jnp.dot(w_ref[...], value, preferred_element_type=F32)
            for i in range(2):
                turned[pl.ds(at + i, 2 * size, stride=pitch), :] = result[
                    :, i * LANES : (i + 1) * LANES
                ]
        per_group = size // len(outs)
        for k, piece in enumerate(outs):
            group = mine_ref[0] ^ k
            for d in range(2):
                for j in range(per_group):
                    line = (d * size + group * per_group + j) * pitch
                    piece[d, :, j * LANES : (j + 1) * LANES] = turned[
                        pl.ds(line, len(held)), :
                    ].astype(BF16)


def image_rows(own, own_at, rows, rim, rim_at, factors, part, shift, mine, groups, before):
    _, subs, _, _, tile, size = own.shape
    finish = mine is not None
    table, turn_cos, turn_sin = doppler_tables(size, 1)
    outer = as_bf16(realified(table))
    inner = as_bf16(realified(table).T)
    whole = lambda *shape: pl.BlockSpec(shape, lambda i: (0,) * len(shape))
    lines = pl.BlockSpec((tile, size), lambda i: (i, 0))
    width = size * size // groups
    in_specs = [
        pl.BlockSpec((1, subs, rows, 2, tile, size), lambda i: (i, 0, own_at, 0, 0, 0)),
        pl.BlockSpec((1, subs, MAXS, 2, tile, size), lambda i: (i, 0, rim_at, 0, 0, 0)),
        pl.BlockSpec((1, subs, rows, 2, tile, size), lambda i: (i, 0, part, 0, 0, 0)),
        lines,
        lines,
        lines,
        whole(2 * size, 2 * size),
    ]
    operands = [own, rim, factors, shift, turn_cos, turn_sin, inner]
    scratch = [
        pltpu.VMEM((subs, 2, rows, tile, size), BF16),
        pltpu.VMEM((rows * tile, 2 * size), BF16),
    ]
    if finish:
        total = rows + sum(piece.shape[0] for piece in before)
        in_specs += [pl.BlockSpec(memory_space=pltpu.SMEM), whole(2 * size, 2 * size)]
        in_specs += [whole(*piece.shape) for piece in before]
        operands += [mine, outer, *before]
        out_specs = [whole(2, total, width)] * groups
        out_shape = [jax.ShapeDtypeStruct((2, total, width), BF16)] * groups
        scratch += [
            pltpu.VMEM((rows, 2, size, size), BF16),
            pltpu.VMEM((2 * size * (total + 1), LANES), F32),
        ]
    else:
        out_specs = pl.BlockSpec((rows, 2, tile, size), lambda i: (0, 0, i, 0))
        out_shape = jax.ShapeDtypeStruct((rows, 2, size, size), BF16)
    return pl.pallas_call(
        functools.partial(image_kernel, len(before), finish),
        grid=(size // tile,),
        in_specs=in_specs,
        out_specs=out_specs,
        out_shape=out_shape,
        scratch_shapes=scratch,
        compiler_params=pltpu.CompilerParams(vmem_limit_bytes=VMEM),
        name="image_rows",
    )(*operands)


def place_kernel(mine_ref, *refs):
    pieces, o_ref = refs[:-1], refs[-1]
    rows = pieces[0].shape[1]
    groups = len(pieces) // 2
    for half in range(2):
        for k in range(groups):
            line = (mine_ref[0] ^ k) * 2 * rows + half * rows
            o_ref[0, pl.ds(pl.multiple_of(line, rows), rows), :] = pieces[half * groups + k][0]


def place_rows(mine, pieces):
    _, rows, width = pieces[0].shape
    return pl.pallas_call(
        place_kernel,
        grid=(2,),
        in_specs=[pl.BlockSpec(memory_space=pltpu.SMEM)]
        + [pl.BlockSpec((1, rows, width), lambda i: (i, 0, 0))] * len(pieces),
        out_specs=pl.BlockSpec((1, rows * len(pieces), width), lambda i: (i, 0, 0)),
        out_shape=jax.ShapeDtypeStruct((2, rows * len(pieces), width), BF16),
        compiler_params=pltpu.CompilerParams(vmem_limit_bytes=VMEM),
        name="place_rows",
    )(mine, *pieces)


def on_device(raw_echo, range_phase, kappa, doppler, migration):
    _, _, range_len, pulse_dev = raw_echo.shape
    puls, subs = lax.axis_size("pul"), lax.axis_size("sub")
    blocks = puls * subs
    rows = range_len // blocks
    half = rows // 2
    pulse_len = pulse_dev * puls
    size = math.isqrt(pulse_len)
    sub_index = lax.axis_index("sub")
    mine = sub_index.reshape(1).astype(jnp.int32)
    middle = range_middle(range_phase, math.isqrt(range_len))
    echo = raw_echo.reshape(2, range_len, pulse_dev)

    def spread(sent):
        got = lax.all_to_all(sent, ("pul", "sub"), 0, 0, tiled=True)
        return got.reshape((puls, subs) + sent.shape[1:])

    def swap(pieces):
        sent = [
            lax.ppermute(pieces[k], "sub", [(i, i ^ k) for i in range(subs)])
            for k in range(subs - 1, 0, -1)
        ]
        return [pieces[0]] + sent[::-1]

    (sent,) = range_compress(echo, middle, 0, 1, blocks, 1)
    sent, echo = lax.optimization_barrier((sent, echo))
    first = spread(sent)
    count = pulse_dev // LANES - 1
    sent_low, sent_high = range_compress(echo, middle, 1, count, blocks, 2)
    own_shift = lax.dynamic_slice_in_dim(migration, sub_index, 1, 0)
    shift = own_shift.reshape(size, size).T
    phase = jnp.swapaxes(doppler.reshape(subs, size, size), 1, 2) * (0.5 / math.pi)
    own_kappa = lax.dynamic_slice_in_dim(kappa, sub_index * rows, rows, 0)
    first, sent_low, phase, own_kappa, shift = lax.optimization_barrier(
        (first, sent_low, phase, own_kappa, shift)
    )
    got_low = spread(sent_low)
    got_low, sent_high = lax.optimization_barrier((got_low, sent_high))
    got_high = spread(sent_high)
    low, edge = doppler_forward(first, got_low, 0, half, size, True)
    low, own_kappa = lax.optimization_barrier((low, own_kappa))
    factors = azimuth_factors(own_kappa, phase)
    place = lambda block: (block % subs) * puls + block // subs
    pairs = [(place(block), place(block - 1)) for block in range(1, blocks)]
    top = image_rows(low, 0, MAXS, low, 1, factors, 0, shift, None, subs, [])
    got_high, top, edge = lax.optimization_barrier((got_high, top, edge))
    rim = lax.ppermute(edge, ("sub", "pul"), pairs)
    (high,) = doppler_forward(first, got_high, 1, half, size, False)
    pieces = image_rows(low, 1, MAXS, high, 0, factors, 1, shift, mine, subs, [top])
    upper = swap(pieces)
    pieces = image_rows(high, 0, half, rim, 0, factors, 1, shift, mine, subs, [])
    lower = swap(pieces)
    return place_rows(mine, upper + lower)


def solution(mesh):
    placed = (P(None, "sub", None, "pul"), P(), P("pul"), P(), P("pul", None))
    return jax.shard_map(
        on_device, mesh=mesh, in_specs=placed, out_specs=P(None, "pul", "sub"), check_vma=False
    )
```

```python
import functools
import math

import jax
import jax.numpy as jnp
import numpy as np
from jax import lax
from jax.experimental import pallas as pl
from jax.experimental.pallas import tpu as pltpu
from jax.sharding import PartitionSpec as P

MAXS = 8
RBLK = 32
LANES = 128
UNROLL = 4
TILE = 32
VMEM = 56 * 1024 * 1024
F32 = jnp.float32
BF16 = jnp.bfloat16


def realified(table):
    return np.block([[table.real, -table.imag], [table.imag, table.real]])


def unit_table(rows, cols, length, direction):
    product = np.outer(np.asarray(rows), np.asarray(cols)) % length
    return np.exp(direction * 2j * np.pi * product / length)


def as_bf16(table):
    return np.asarray(table, np.float32).astype(BF16)


def middle_kernel(phase_ref, wave_ref, o_ref):
    cosine, sine = turns(phase_ref[...])
    size = phase_ref.shape[1] // 2
    lane = lax.broadcasted_iota(jnp.int32, sine.shape, 1)
    sine = jnp.where(lane < size, sine, -sine)
    for k2 in range(o_ref.shape[0]):
        wave = wave_ref[k2].astype(F32)
        left = wave * cosine[k2 : k2 + 1] + pltpu.roll(wave, size, 1) * sine[k2 : k2 + 1]
        o_ref[k2] = lax.dot_general(
            left.astype(BF16),
            wave_ref[k2],
            (((1,), (1,)), ((), ())),
            preferred_element_type=F32,
        ).astype(BF16)


def range_middle(range_phase, size):
    length = size * size
    k2 = np.arange(size)[:, None, None]
    j1 = np.arange(size)[None, :, None]
    k1 = np.arange(size)[None, None, :]
    wave = np.exp(2j * np.pi * ((j1 * (k2 + size * k1)) % length) / length) / size
    wave = as_bf16(np.stack([realified(wave[k]) for k in range(size)]))
    phase = range_phase.reshape(size, size).T * (0.5 / math.pi)
    group = 16
    block = pl.BlockSpec((group, 2 * size, 2 * size), lambda i: (i, 0, 0))
    return pl.pallas_call(
        middle_kernel,
        grid=(size // group,),
        in_specs=[pl.BlockSpec((group, 2 * size), lambda i: (i, 0)), block],
        out_specs=block,
        out_shape=jax.ShapeDtypeStruct(wave.shape, BF16),
        compiler_params=pltpu.CompilerParams(vmem_limit_bytes=VMEM),
        name="range_middle",
    )(jnp.concatenate([phase, phase], axis=1), wave)


def range_kernel(size, splits, x_ref, w_ref, t_ref, v_ref, *refs):
    outs, (one, two) = refs[:splits], refs[splits:]
    both = 2 * size
    pitch = size + 1

    def cast(step, carry):
        for u in range(8):
            line = step * 8 + u
            for c in range(2):
                one[pl.ds((c * size + line) * pitch, size), :] = x_ref[
                    c, pl.ds(pl.multiple_of(line * size, size), size), :
                ].astype(F32)
        return carry

    lax.fori_loop(0, size // 8, cast, 0)

    def strided(source, target, table):
        def body(step, carry):
            for u in range(UNROLL):
                j1 = (step * UNROLL + u) * 2
                value = jnp.concatenate(
                    [source[pl.ds(j1 + i, both, stride=pitch), :] for i in range(2)], axis=1
                ).astype(BF16)
                out = jnp.dot(table, value, preferred_element_type=F32)
                for i in range(2):
                    target[pl.ds(j1 + i, both, stride=pitch), :] = out[
                        :, i * LANES : (i + 1) * LANES
                    ]
            return carry

        lax.fori_loop(0, size // (2 * UNROLL), body, 0)

    strided(one, two, w_ref[...])

    def inner(step, carry):
        for u in range(2 * UNROLL):
            k2 = step * 2 * UNROLL + u
            value = jnp.concatenate(
                [two[pl.ds((c * size + k2) * pitch, size), :] for c in range(2)], axis=0
            ).astype(BF16)
            out = jnp.dot(t_ref[k2], value, preferred_element_type=F32)
            for d in range(2):
                one[pl.ds((d * size + k2) * pitch, size), :] = out[d * size : (d + 1) * size]
        return carry

    lax.fori_loop(0, size // (2 * UNROLL), inner, 0)
    strided(one, two, v_ref[...])
    rows = outs[0].shape[2]
    pieces = size // rows

    def give(step, carry):
        for u in range(8):
            line = step * 8 + u
            for piece in range(pieces):
                block = line * (pieces // splits) + piece // splits
                for d in range(2):
                    outs[piece % splits][block, d] = two[
                        pl.ds((d * size + line) * pitch + piece * rows, rows), :
                    ].astype(BF16)
        return carry

    lax.fori_loop(0, size // 8, give, 0)


def range_compress(echo, middle, first, count, blocks, splits):
    length = echo.shape[1]
    size = math.isqrt(length)
    index = np.arange(size)
    forward = as_bf16(realified(unit_table(index, index, size, -1)))
    backward = as_bf16(realified(unit_table(index, index, size, 1)))
    rows = length // blocks // splits
    whole = lambda *shape: pl.BlockSpec(shape, lambda i: (0,) * len(shape))
    scratch = pltpu.VMEM((2 * (length + size), LANES), F32)
    return pl.pallas_call(
        functools.partial(range_kernel, size, splits),
        grid=(count,),
        in_specs=[
            pl.BlockSpec((2, length, LANES), lambda i: (0, 0, first + i)),
            whole(2 * size, 2 * size),
            whole(size, 2 * size, 2 * size),
            whole(2 * size, 2 * size),
        ],
        out_specs=[pl.BlockSpec((blocks, 2, rows, LANES), lambda i: (0, 0, 0, i))] * splits,
        out_shape=[jax.ShapeDtypeStruct((blocks, 2, rows, count * LANES), BF16)] * splits,
        scratch_shapes=[scratch, scratch],
        compiler_params=pltpu.CompilerParams(vmem_limit_bytes=VMEM),
        name="range_compress",
    )(echo, forward, middle, backward)


def doppler_kernel(rows, first, rest, w_ref, cos_ref, sin_ref, u_ref, o_ref, *refs):
    held = refs[-1]
    sources = first.shape[0]
    size = cos_ref.shape[0]
    lines = size // sources
    early = first.shape[4] // LANES
    pitch = rows + 1

    def cast(source, carry):
        for line in range(lines):
            for c in range(2):
                part, at = (first, line) if line < early else (rest, line - early)
                value = part[source, 0, c, :, at * LANES : (at + 1) * LANES]
                base = (c * lines + line) * sources
                held[pl.ds((base + source) * pitch, rows), :] = value.astype(F32)
        return carry

    lax.fori_loop(0, sources, cast, 0)

    def pair(first_row):
        value = jnp.concatenate(
            [held[pl.ds(first_row + i, 2 * size, stride=pitch), :] for i in range(2)], axis=1
        ).astype(BF16)
        first = jnp.dot(w_ref[...], value, preferred_element_type=F32)
        stacked = []
        for i in range(2):
            real = first[:size, i * LANES : (i + 1) * LANES]
            imag = first[size:, i * LANES : (i + 1) * LANES]
            stacked.append(
                jnp.concatenate(
                    [
                        real * cos_ref[...] - imag * sin_ref[...],
                        real * sin_ref[...] + imag * cos_ref[...],
                    ],
                    axis=1,
                ).astype(BF16)
            )
        second = jnp.dot(
            jnp.concatenate(stacked, axis=0), u_ref[...], preferred_element_type=F32
        ).astype(BF16)
        for i in range(2):
            for d in range(2):
                for tile in range(size // TILE):
                    line = i * size + tile * TILE
                    value = second[line : line + TILE, d * LANES : (d + 1) * LANES]
                    o_ref[tile, 0, first_row + i, d] = value

    def body(step, carry):
        for u in range(4):
            pair(step * 8 + 2 * u)
        return carry

    lax.fori_loop(0, rows // 8, body, 0)
    for rim in refs[:-1]:
        rim[:, 0] = o_ref[:, 0, :MAXS]


def doppler_tables(size, direction):
    index = np.arange(size)
    table = unit_table(index, index, size, direction)
    turn = unit_table(index, index, size * size, direction) / size
    return table, turn.real.astype(np.float32), turn.imag.astype(np.float32)


def doppler_forward(first, rest, part, rows, size, with_rim):
    sources, subs, _, _, width = rest.shape
    table, turn_cos, turn_sin = doppler_tables(size, -1)
    lines = size // sources
    order = np.asarray(
        [lines * source + line for line in range(lines) for source in range(sources)]
    )
    outer = as_bf16(realified(table[:, order]))
    inner = as_bf16(realified(table).T)
    whole = lambda *shape: pl.BlockSpec(shape, lambda i: (0,) * len(shape))
    heights = [rows, MAXS] if with_rim else [rows]
    return pl.pallas_call(
        functools.partial(doppler_kernel, rows),
        grid=(subs,),
        in_specs=[
            pl.BlockSpec(
                (sources, 1, 2, rows, first.shape[4]), lambda i: (0, i, 0, part, 0)
            ),
            pl.BlockSpec((sources, 1, 2, rows, width), lambda i: (0, i, 0, 0, 0)),
            whole(2 * size, 2 * size),
            whole(size, size),
            whole(size, size),
            whole(2 * size, 2 * size),
        ],
        out_specs=[
            pl.BlockSpec((size // TILE, 1, height, 2, TILE, size), lambda i: (0, i, 0, 0, 0, 0))
            for height in heights
        ],
        out_shape=[
            jax.ShapeDtypeStruct((size // TILE, subs, height, 2, TILE, size), BF16)
            for height in heights
        ],
        scratch_shapes=[pltpu.VMEM((2 * size * (rows + 1), LANES), F32)],
        compiler_params=pltpu.CompilerParams(vmem_limit_bytes=VMEM),
        name="doppler_forward",
    )(first, rest, outer, turn_cos, turn_sin, inner)


def turn_polynomials():
    nodes = 0.25 * (1 - np.cos((np.arange(64) + 0.5) * np.pi / 64)) / 2
    roots = np.sqrt(nodes)
    sine = np.polynomial.polynomial.polyfit(nodes, np.sin(2 * np.pi * roots) / roots, 6)
    cosine = np.polynomial.polynomial.polyfit(nodes, np.cos(2 * np.pi * roots), 6)
    return [round(float(v), 7) for v in sine], [round(float(v), 7) for v in cosine]


def turns(cycles):
    sine_terms, cosine_terms = turn_polynomials()
    part = cycles - jnp.floor(cycles + 0.5)
    square = part * part
    sine = jnp.full_like(square, sine_terms[-1])
    cosine = jnp.full_like(square, cosine_terms[-1])
    for term in reversed(sine_terms[:-1]):
        sine = sine * square + term
    for term in reversed(cosine_terms[:-1]):
        cosine = cosine * square + term
    return cosine, sine * part


def factor_kernel(kappa_ref, phase_ref, o_ref):
    def body(step, carry):
        for u in range(2):
            row = step * 2 + u
            for tile in range(o_ref.shape[0]):
                cosine, sine = turns(kappa_ref[row] * phase_ref[0, tile * TILE : (tile + 1) * TILE])
                o_ref[tile, 0, row, 0] = cosine.astype(BF16)
                o_ref[tile, 0, row, 1] = sine.astype(BF16)
        return carry

    lax.fori_loop(0, o_ref.shape[2] // 2, body, 0)


def azimuth_factors(kappa, phase):
    subs, size, _ = phase.shape
    rows = kappa.shape[0]
    return pl.pallas_call(
        factor_kernel,
        grid=(subs,),
        in_specs=[
            pl.BlockSpec(memory_space=pltpu.SMEM),
            pl.BlockSpec((1, size, size), lambda i: (i, 0, 0)),
        ],
        out_specs=pl.BlockSpec(
            (size // TILE, 1, rows, 2, TILE, size), lambda i: (0, i, 0, 0, 0, 0)
        ),
        out_shape=jax.ShapeDtypeStruct((size // TILE, subs, rows, 2, TILE, size), BF16),
        compiler_params=pltpu.CompilerParams(vmem_limit_bytes=VMEM),
        name="azimuth_factors",
    )(kappa, phase)


def image_kernel(earlier, finish, *refs):
    own, rim, factor_ref, shift_ref, cos_ref, sin_ref, u_ref = refs[:7]
    refs = refs[7:]
    if finish:
        mine_ref, w_ref = refs[:2]
        before, refs = refs[2 : 2 + earlier], refs[2 + earlier :]
        outs, (moved, summed, middle, turned) = refs[:-4], refs[-4:]
    else:
        (out, moved, summed) = refs
    step = pl.program_id(0)
    _, subs, rows, _, tile, size = own.shape
    shift = shift_ref[...]
    bits = [((shift >> k) & 1).astype(F32).astype(BF16) > 0.5 for k in range(4)]

    def aperture(index, carry):
        for d in range(2):
            values = [own[0, index, r, d] for r in range(rows)]
            values += [rim[0, index, r, d] for r in range(MAXS)]
            four = [jnp.where(bits[2], values[r + 4], values[r]) for r in range(rows + 3)]
            two = [jnp.where(bits[1], four[r + 2], four[r]) for r in range(rows + 1)]
            one = [jnp.where(bits[0], two[r + 1], two[r]) for r in range(rows)]
            for r in range(rows):
                moved[index, d, r] = jnp.where(bits[3], values[r + 8], one[r])
        return carry

    lax.fori_loop(0, subs, aperture, 0)

    def row_sum(turn, carry):
        for u in range(4):
            row = turn * 4 + u
            real = jnp.zeros((tile, size), F32)
            imag = jnp.zeros((tile, size), F32)
            for index in range(subs):
                cosine = factor_ref[0, index, row, 0].astype(F32)
                sine = factor_ref[0, index, row, 1].astype(F32)
                a, b = moved[index, 0, row].astype(F32), moved[index, 1, row].astype(F32)
                real = real + (a * cosine - b * sine)
                imag = imag + (a * sine + b * cosine)
            summed[pl.ds(pl.multiple_of(row * tile, tile), tile), :] = jnp.concatenate(
                [real, imag], axis=1
            ).astype(BF16)
        return carry

    lax.fori_loop(0, rows // 4, row_sum, 0)
    first = jnp.dot(summed[...], u_ref[...], preferred_element_type=F32)
    for r in range(rows):
        real = first[r * tile : (r + 1) * tile, :size]
        imag = first[r * tile : (r + 1) * tile, size:]
        real, imag = (
            (real * cos_ref[...] - imag * sin_ref[...]).astype(BF16),
            (real * sin_ref[...] + imag * cos_ref[...]).astype(BF16),
        )
        if finish:
            where = pl.ds(pl.multiple_of(step * tile, tile), tile)
            middle[r, 0, where, :] = real
            middle[r, 1, where, :] = imag
        else:
            out[r, 0] = real
            out[r, 1] = imag

    if not finish:
        return

    @pl.when(step == pl.num_programs(0) - 1)
    def _():
        held = [(ref, r) for ref in list(before) + [middle] for r in range(ref.shape[0])]
        pitch = len(held) + 1
        for at in range(0, len(held), 2):
            value = jnp.concatenate(
                [
                    jnp.concatenate([ref[r, c] for c in range(2)], axis=0)
                    for ref, r in held[at : at + 2]
                ],
                axis=1,
            )
            result = jnp.dot(w_ref[...], value, preferred_element_type=F32)
            for i in range(2):
                turned[pl.ds(at + i, 2 * size, stride=pitch), :] = result[
                    :, i * LANES : (i + 1) * LANES
                ]
        per_group = size // len(outs)
        for k, piece in enumerate(outs):
            group = mine_ref[0] ^ k
            for d in range(2):
                for j in range(per_group):
                    line = (d * size + group * per_group + j) * pitch
                    piece[d, :, j * LANES : (j + 1) * LANES] = turned[
                        pl.ds(line, len(held)), :
                    ].astype(BF16)


def image_rows(own, own_at, rows, rim, rim_at, factors, part, shift, mine, groups, before):
    _, subs, _, _, tile, size = own.shape
    finish = mine is not None
    table, turn_cos, turn_sin = doppler_tables(size, 1)
    outer = as_bf16(realified(table))
    inner = as_bf16(realified(table).T)
    whole = lambda *shape: pl.BlockSpec(shape, lambda i: (0,) * len(shape))
    lines = pl.BlockSpec((tile, size), lambda i: (i, 0))
    width = size * size // groups
    in_specs = [
        pl.BlockSpec((1, subs, rows, 2, tile, size), lambda i: (i, 0, own_at, 0, 0, 0)),
        pl.BlockSpec((1, subs, MAXS, 2, tile, size), lambda i: (i, 0, rim_at, 0, 0, 0)),
        pl.BlockSpec((1, subs, rows, 2, tile, size), lambda i: (i, 0, part, 0, 0, 0)),
        lines,
        lines,
        lines,
        whole(2 * size, 2 * size),
    ]
    operands = [own, rim, factors, shift, turn_cos, turn_sin, inner]
    scratch = [
        pltpu.VMEM((subs, 2, rows, tile, size), BF16),
        pltpu.VMEM((rows * tile, 2 * size), BF16),
    ]
    if finish:
        total = rows + sum(piece.shape[0] for piece in before)
        in_specs += [pl.BlockSpec(memory_space=pltpu.SMEM), whole(2 * size, 2 * size)]
        in_specs += [whole(*piece.shape) for piece in before]
        operands += [mine, outer, *before]
        out_specs = [whole(2, total, width)] * groups
        out_shape = [jax.ShapeDtypeStruct((2, total, width), BF16)] * groups
        scratch += [
            pltpu.VMEM((rows, 2, size, size), BF16),
            pltpu.VMEM((2 * size * (total + 1), LANES), F32),
        ]
    else:
        out_specs = pl.BlockSpec((rows, 2, tile, size), lambda i: (0, 0, i, 0))
        out_shape = jax.ShapeDtypeStruct((rows, 2, size, size), BF16)
    return pl.pallas_call(
        functools.partial(image_kernel, len(before), finish),
        grid=(size // tile,),
        in_specs=in_specs,
        out_specs=out_specs,
        out_shape=out_shape,
        scratch_shapes=scratch,
        compiler_params=pltpu.CompilerParams(vmem_limit_bytes=VMEM),
        name="image_rows",
    )(*operands)


def place_kernel(mine_ref, *refs):
    pieces, o_ref = refs[:-1], refs[-1]
    rows = pieces[0].shape[1]
    groups = len(pieces) // 2
    for half in range(2):
        for k in range(groups):
            line = (mine_ref[0] ^ k) * 2 * rows + half * rows
            o_ref[0, pl.ds(pl.multiple_of(line, rows), rows), :] = pieces[half * groups + k][0]


def place_rows(mine, pieces):
    _, rows, width = pieces[0].shape
    return pl.pallas_call(
        place_kernel,
        grid=(2,),
        in_specs=[pl.BlockSpec(memory_space=pltpu.SMEM)]
        + [pl.BlockSpec((1, rows, width), lambda i: (i, 0, 0))] * len(pieces),
        out_specs=pl.BlockSpec((1, rows * len(pieces), width), lambda i: (i, 0, 0)),
        out_shape=jax.ShapeDtypeStruct((2, rows * len(pieces), width), BF16),
        compiler_params=pltpu.CompilerParams(vmem_limit_bytes=VMEM),
        name="place_rows",
    )(mine, *pieces)


def on_device(raw_echo, range_phase, kappa, doppler, migration):
    _, _, range_len, pulse_dev = raw_echo.shape
    puls, subs = lax.axis_size("pul"), lax.axis_size("sub")
    blocks = puls * subs
    rows = range_len // blocks
    half = rows // 2
    pulse_len = pulse_dev * puls
    size = math.isqrt(pulse_len)
    sub_index = lax.axis_index("sub")
    mine = sub_index.reshape(1).astype(jnp.int32)
    middle = range_middle(range_phase, math.isqrt(range_len))
    echo = raw_echo.reshape(2, range_len, pulse_dev)

    def spread(sent):
        got = lax.all_to_all(sent, ("pul", "sub"), 0, 0, tiled=True)
        return got.reshape((puls, subs) + sent.shape[1:])

    def swap(pieces):
        sent = [
            lax.ppermute(pieces[k], "sub", [(i, i ^ k) for i in range(subs)])
            for k in range(subs - 1, 0, -1)
        ]
        return [pieces[0]] + sent[::-1]

    early = pulse_dev // LANES // 2
    (sent,) = range_compress(echo, middle, 0, early, blocks, 1)
    sent, echo = lax.optimization_barrier((sent, echo))
    first = spread(sent)
    count = pulse_dev // LANES - early
    sent_low, sent_high = range_compress(echo, middle, early, count, blocks, 2)
    own_shift = lax.dynamic_slice_in_dim(migration, sub_index, 1, 0)
    shift = own_shift.reshape(size, size).T
    phase = jnp.swapaxes(doppler.reshape(subs, size, size), 1, 2) * (0.5 / math.pi)
    own_kappa = lax.dynamic_slice_in_dim(kappa, sub_index * rows, rows, 0)
    factors = azimuth_factors(own_kappa, phase)
    first, sent_low, factors, shift = lax.optimization_barrier((first, sent_low, factors, shift))
    got_low = spread(sent_low)
    got_low, sent_high = lax.optimization_barrier((got_low, sent_high))
    got_high = spread(sent_high)
    low, edge = doppler_forward(first, got_low, 0, half, size, True)
    place = lambda block: (block % subs) * puls + block // subs
    pairs = [(place(block), place(block - 1)) for block in range(1, blocks)]
    rim = lax.ppermute(edge, ("sub", "pul"), pairs)
    top = image_rows(low, 0, MAXS, low, 1, factors, 0, shift, None, subs, [])
    got_high, top = lax.optimization_barrier((got_high, top))
    (high,) = doppler_forward(first, got_high, 1, half, size, False)
    pieces = image_rows(low, 1, MAXS, high, 0, factors, 1, shift, mine, subs, [top])
    upper = swap(pieces)
    pieces = image_rows(high, 0, half, rim, 0, factors, 1, shift, mine, subs, [])
    lower = swap(pieces)
    return place_rows(mine, upper + lower)


def solution(mesh):
    placed = (P(None, "sub", None, "pul"), P(), P("pul"), P(), P("pul", None))
    return jax.shard_map(
        on_device, mesh=mesh, in_specs=placed, out_specs=P(None, "pul", "sub"), check_vma=False
    )
```

```python
import functools
import math

import jax
import jax.numpy as jnp
import numpy as np
from jax import lax
from jax.experimental import pallas as pl
from jax.experimental.pallas import tpu as pltpu
from jax.sharding import PartitionSpec as P

MAXS = 8
RBLK = 32
LANES = 128
RANGE_UNROLL = 8
TILE = 64
VMEM = 56 * 1024 * 1024
F32 = jnp.float32
BF16 = jnp.bfloat16


def realified(table):
    return np.block([[table.real, -table.imag], [table.imag, table.real]])


def unit_table(rows, cols, length, direction):
    product = np.outer(np.asarray(rows), np.asarray(cols)) % length
    return np.exp(direction * 2j * np.pi * product / length)


def as_bf16(table):
    return np.asarray(table, np.float32).astype(BF16)


def middle_kernel(phase_ref, wave_ref, o_ref):
    cosine, sine = turns(phase_ref[...])
    size = phase_ref.shape[1] // 2
    lane = lax.broadcasted_iota(jnp.int32, sine.shape, 1)
    sine = jnp.where(lane < size, sine, -sine)
    for k2 in range(o_ref.shape[0]):
        wave = wave_ref[k2].astype(F32)
        left = wave * cosine[k2 : k2 + 1] + pltpu.roll(wave, size, 1) * sine[k2 : k2 + 1]
        o_ref[k2] = lax.dot_general(
            left.astype(BF16),
            wave_ref[k2],
            (((1,), (1,)), ((), ())),
            preferred_element_type=F32,
        ).astype(BF16)


def range_middle(range_phase, size):
    length = size * size
    k2 = np.arange(size)[:, None, None]
    j1 = np.arange(size)[None, :, None]
    k1 = np.arange(size)[None, None, :]
    wave = np.exp(2j * np.pi * ((j1 * (k2 + size * k1)) % length) / length) / size
    wave = as_bf16(np.stack([realified(wave[k]) for k in range(size)]))
    phase = range_phase.reshape(size, size).T * (0.5 / math.pi)
    group = 32
    block = pl.BlockSpec((group, 2 * size, 2 * size), lambda i: (i, 0, 0))
    return pl.pallas_call(
        middle_kernel,
        grid=(size // group,),
        in_specs=[pl.BlockSpec((group, 2 * size), lambda i: (i, 0)), block],
        out_specs=block,
        out_shape=jax.ShapeDtypeStruct(wave.shape, BF16),
        compiler_params=pltpu.CompilerParams(vmem_limit_bytes=VMEM),
        name="range_middle",
    )(jnp.concatenate([phase, phase], axis=1), wave)


def range_kernel(size, splits, x_ref, w_ref, t_ref, v_ref, *refs):
    outs, (one, two) = refs[:splits], refs[splits:]
    halves = x_ref.shape[2] // LANES
    both = 2 * size
    pitch = size + 1

    def lanes(h):
        return slice(h * LANES, (h + 1) * LANES)

    def cast(step, carry):
        for u in range(4):
            line = step * 4 + u
            for h in range(halves):
                for c in range(2):
                    one[h, pl.ds((c * size + line) * pitch, size), :] = x_ref[
                        c, pl.ds(pl.multiple_of(line * size, size), size), lanes(h)
                    ].astype(F32)
        return carry

    lax.fori_loop(0, size // 4, cast, 0)

    def strided(source, target, table):
        def body(step, carry):
            for u in range(RANGE_UNROLL):
                j1 = step * RANGE_UNROLL + u
                value = jnp.concatenate(
                    [source[h, pl.ds(j1, both, stride=pitch), :] for h in range(halves)], axis=1
                ).astype(BF16)
                out = jnp.dot(table, value, preferred_element_type=F32)
                for h in range(halves):
                    target[h, pl.ds(j1, both, stride=pitch), :] = out[:, lanes(h)]
            return carry

        lax.fori_loop(0, size // RANGE_UNROLL, body, 0)

    strided(one, two, w_ref[...])

    def inner(step, carry):
        for u in range(RANGE_UNROLL):
            k2 = step * RANGE_UNROLL + u
            value = jnp.concatenate(
                [
                    jnp.concatenate(
                        [two[h, pl.ds((c * size + k2) * pitch, size), :] for c in range(2)], axis=0
                    )
                    for h in range(halves)
                ],
                axis=1,
            ).astype(BF16)
            out = jnp.dot(t_ref[k2], value, preferred_element_type=F32)
            for h in range(halves):
                for d in range(2):
                    one[h, pl.ds((d * size + k2) * pitch, size), :] = out[
                        d * size : (d + 1) * size, lanes(h)
                    ]
        return carry

    lax.fori_loop(0, size // RANGE_UNROLL, inner, 0)
    strided(one, two, v_ref[...])
    rows = outs[0].shape[2]
    pieces = size // rows

    def give(step, carry):
        for u in range(4):
            line = step * 4 + u
            for piece in range(pieces):
                block = line * (pieces // splits) + piece // splits
                for d in range(2):
                    for h in range(halves):
                        outs[piece % splits][block, d, :, lanes(h)] = two[
                            h, pl.ds((d * size + line) * pitch + piece * rows, rows), :
                        ].astype(BF16)
        return carry

    lax.fori_loop(0, size // 4, give, 0)


def range_compress(echo, middle, chunk, width, blocks, splits):
    length = echo.shape[1]
    size = math.isqrt(length)
    index = np.arange(size)
    forward = as_bf16(realified(unit_table(index, index, size, -1)))
    backward = as_bf16(realified(unit_table(index, index, size, 1)))
    rows = length // blocks // splits
    whole = lambda *shape: pl.BlockSpec(shape, lambda i: (0,) * len(shape))
    scratch = pltpu.VMEM((width // LANES, 2 * (length + size), LANES), F32)
    return pl.pallas_call(
        functools.partial(range_kernel, size, splits),
        grid=(1,),
        in_specs=[
            pl.BlockSpec((2, length, width), lambda i: (0, 0, chunk)),
            whole(2 * size, 2 * size),
            whole(size, 2 * size, 2 * size),
            whole(2 * size, 2 * size),
        ],
        out_specs=[whole(blocks, 2, rows, width)] * splits,
        out_shape=[jax.ShapeDtypeStruct((blocks, 2, rows, width), BF16)] * splits,
        scratch_shapes=[scratch, scratch],
        compiler_params=pltpu.CompilerParams(vmem_limit_bytes=VMEM),
        name="range_compress",
    )(echo, forward, middle, backward)


def doppler_kernel(rows, first, rest, w_ref, cos_ref, sin_ref, u_ref, o_ref, *refs):
    held = refs[-1]
    sources = first.shape[0]
    size = cos_ref.shape[0]
    lines = size // sources
    early = first.shape[4] // LANES
    pitch = rows + 1

    def cast(source, carry):
        for line in range(lines):
            for c in range(2):
                part, at = (first, line) if line < early else (rest, line - early)
                value = part[source, 0, c, :, at * LANES : (at + 1) * LANES]
                base = (c * lines + line) * sources
                held[pl.ds((base + source) * pitch, rows), :] = value.astype(F32)
        return carry

    lax.fori_loop(0, sources, cast, 0)

    def pair(first_row):
        value = jnp.concatenate(
            [held[pl.ds(first_row + i, 2 * size, stride=pitch), :] for i in range(2)], axis=1
        ).astype(BF16)
        first = jnp.dot(w_ref[...], value, preferred_element_type=F32)
        stacked = []
        for i in range(2):
            real = first[:size, i * LANES : (i + 1) * LANES]
            imag = first[size:, i * LANES : (i + 1) * LANES]
            stacked.append(
                jnp.concatenate(
                    [
                        real * cos_ref[...] - imag * sin_ref[...],
                        real * sin_ref[...] + imag * cos_ref[...],
                    ],
                    axis=1,
                ).astype(BF16)
            )
        second = jnp.dot(
            jnp.concatenate(stacked, axis=0), u_ref[...], preferred_element_type=F32
        ).astype(BF16)
        for i in range(2):
            for d in range(2):
                for tile in range(size // TILE):
                    line = i * size + tile * TILE
                    value = second[line : line + TILE, d * LANES : (d + 1) * LANES]
                    o_ref[tile, 0, first_row + i, d] = value

    for first_row in range(0, rows, 2):
        pair(first_row)
    for rim in refs[:-1]:
        rim[:, 0] = o_ref[:, 0, :MAXS]


def doppler_tables(size, direction):
    index = np.arange(size)
    table = unit_table(index, index, size, direction)
    turn = unit_table(index, index, size * size, direction) / size
    return table, turn.real.astype(np.float32), turn.imag.astype(np.float32)


def doppler_forward(first, rest, part, rows, size, with_rim):
    sources, subs, _, _, width = rest.shape
    table, turn_cos, turn_sin = doppler_tables(size, -1)
    lines = size // sources
    order = np.asarray(
        [lines * source + line for line in range(lines) for source in range(sources)]
    )
    outer = as_bf16(realified(table[:, order]))
    inner = as_bf16(realified(table).T)
    whole = lambda *shape: pl.BlockSpec(shape, lambda i: (0,) * len(shape))
    heights = [rows, MAXS] if with_rim else [rows]
    return pl.pallas_call(
        functools.partial(doppler_kernel, rows),
        grid=(subs,),
        in_specs=[
            pl.BlockSpec(
                (sources, 1, 2, rows, first.shape[4]), lambda i: (0, i, 0, part, 0)
            ),
            pl.BlockSpec((sources, 1, 2, rows, width), lambda i: (0, i, 0, 0, 0)),
            whole(2 * size, 2 * size),
            whole(size, size),
            whole(size, size),
            whole(2 * size, 2 * size),
        ],
        out_specs=[
            pl.BlockSpec((size // TILE, 1, height, 2, TILE, size), lambda i: (0, i, 0, 0, 0, 0))
            for height in heights
        ],
        out_shape=[
            jax.ShapeDtypeStruct((size // TILE, subs, height, 2, TILE, size), BF16)
            for height in heights
        ],
        scratch_shapes=[pltpu.VMEM((2 * size * (rows + 1), LANES), F32)],
        compiler_params=pltpu.CompilerParams(vmem_limit_bytes=VMEM),
        name="doppler_forward",
    )(first, rest, outer, turn_cos, turn_sin, inner)


def turn_polynomials():
    nodes = 0.25 * (1 - np.cos((np.arange(64) + 0.5) * np.pi / 64)) / 2
    roots = np.sqrt(nodes)
    sine = np.polynomial.polynomial.polyfit(nodes, np.sin(2 * np.pi * roots) / roots, 6)
    cosine = np.polynomial.polynomial.polyfit(nodes, np.cos(2 * np.pi * roots), 6)
    return [round(float(v), 7) for v in sine], [round(float(v), 7) for v in cosine]


def turns(cycles):
    sine_terms, cosine_terms = turn_polynomials()
    part = cycles - jnp.floor(cycles + 0.5)
    square = part * part
    sine = jnp.full_like(square, sine_terms[-1])
    cosine = jnp.full_like(square, cosine_terms[-1])
    for term in reversed(sine_terms[:-1]):
        sine = sine * square + term
    for term in reversed(cosine_terms[:-1]):
        cosine = cosine * square + term
    return cosine, sine * part


def factor_kernel(kappa_ref, phase_ref, o_ref):
    def body(step, carry):
        for u in range(2):
            row = step * 2 + u
            for tile in range(o_ref.shape[0]):
                cosine, sine = turns(kappa_ref[row] * phase_ref[0, tile * TILE : (tile + 1) * TILE])
                o_ref[tile, 0, row, 0] = cosine.astype(BF16)
                o_ref[tile, 0, row, 1] = sine.astype(BF16)
        return carry

    lax.fori_loop(0, o_ref.shape[2] // 2, body, 0)


def azimuth_factors(kappa, phase):
    subs, size, _ = phase.shape
    rows = kappa.shape[0]
    return pl.pallas_call(
        factor_kernel,
        grid=(subs,),
        in_specs=[
            pl.BlockSpec(memory_space=pltpu.SMEM),
            pl.BlockSpec((1, size, size), lambda i: (i, 0, 0)),
        ],
        out_specs=pl.BlockSpec(
            (size // TILE, 1, rows, 2, TILE, size), lambda i: (0, i, 0, 0, 0, 0)
        ),
        out_shape=jax.ShapeDtypeStruct((size // TILE, subs, rows, 2, TILE, size), BF16),
        compiler_params=pltpu.CompilerParams(vmem_limit_bytes=VMEM),
        name="azimuth_factors",
    )(kappa, phase)


def image_kernel(earlier, finish, *refs):
    own, rim, factor_ref, shift_ref, cos_ref, sin_ref, u_ref = refs[:7]
    refs = refs[7:]
    if finish:
        mine_ref, w_ref = refs[:2]
        before, refs = refs[2 : 2 + earlier], refs[2 + earlier :]
        outs, (moved, summed, middle, turned) = refs[:-4], refs[-4:]
    else:
        (out, moved, summed) = refs
    step = pl.program_id(0)
    _, subs, rows, _, tile, size = own.shape
    shift = shift_ref[...]
    bits = [((shift >> k) & 1).astype(F32).astype(BF16) > 0.5 for k in range(4)]

    def aperture(index, carry):
        for d in range(2):
            values = [own[0, index, r, d] for r in range(rows)]
            values += [rim[0, index, r, d] for r in range(MAXS)]
            four = [jnp.where(bits[2], values[r + 4], values[r]) for r in range(rows + 3)]
            two = [jnp.where(bits[1], four[r + 2], four[r]) for r in range(rows + 1)]
            one = [jnp.where(bits[0], two[r + 1], two[r]) for r in range(rows)]
            for r in range(rows):
                moved[index, d, r] = jnp.where(bits[3], values[r + 8], one[r])
        return carry

    lax.fori_loop(0, subs, aperture, 0)

    def row_sum(turn, carry):
        for u in range(4):
            row = turn * 4 + u
            real = jnp.zeros((tile, size), F32)
            imag = jnp.zeros((tile, size), F32)
            for index in range(subs):
                cosine = factor_ref[0, index, row, 0].astype(F32)
                sine = factor_ref[0, index, row, 1].astype(F32)
                a, b = moved[index, 0, row].astype(F32), moved[index, 1, row].astype(F32)
                real = real + (a * cosine - b * sine)
                imag = imag + (a * sine + b * cosine)
            summed[pl.ds(pl.multiple_of(row * tile, tile), tile), :] = jnp.concatenate(
                [real, imag], axis=1
            ).astype(BF16)
        return carry

    lax.fori_loop(0, rows // 4, row_sum, 0)
    first = jnp.dot(summed[...], u_ref[...], preferred_element_type=F32)
    for r in range(rows):
        real = first[r * tile : (r + 1) * tile, :size]
        imag = first[r * tile : (r + 1) * tile, size:]
        real, imag = (
            (real * cos_ref[...] - imag * sin_ref[...]).astype(BF16),
            (real * sin_ref[...] + imag * cos_ref[...]).astype(BF16),
        )
        if finish:
            where = pl.ds(pl.multiple_of(step * tile, tile), tile)
            middle[r, 0, where, :] = real
            middle[r, 1, where, :] = imag
        else:
            out[r, 0] = real
            out[r, 1] = imag

    if not finish:
        return

    @pl.when(step == pl.num_programs(0) - 1)
    def _():
        held = [(ref, r) for ref in list(before) + [middle] for r in range(ref.shape[0])]
        pitch = len(held) + 1
        for at in range(0, len(held), 2):
            value = jnp.concatenate(
                [
                    jnp.concatenate([ref[r, c] for c in range(2)], axis=0)
                    for ref, r in held[at : at + 2]
                ],
                axis=1,
            )
            result = jnp.dot(w_ref[...], value, preferred_element_type=F32)
            for i in range(2):
                turned[pl.ds(at + i, 2 * size, stride=pitch), :] = result[
                    :, i * LANES : (i + 1) * LANES
                ]
        per_group = size // len(outs)
        for k, piece in enumerate(outs):
            group = mine_ref[0] ^ k
            for d in range(2):
                for j in range(per_group):
                    line = (d * size + group * per_group + j) * pitch
                    piece[d, :, j * LANES : (j + 1) * LANES] = turned[
                        pl.ds(line, len(held)), :
                    ].astype(BF16)


def image_rows(own, own_at, rows, rim, rim_at, factors, part, shift, mine, groups, before):
    _, subs, _, _, tile, size = own.shape
    finish = mine is not None
    table, turn_cos, turn_sin = doppler_tables(size, 1)
    outer = as_bf16(realified(table))
    inner = as_bf16(realified(table).T)
    whole = lambda *shape: pl.BlockSpec(shape, lambda i: (0,) * len(shape))
    lines = pl.BlockSpec((tile, size), lambda i: (i, 0))
    width = size * size // groups
    in_specs = [
        pl.BlockSpec((1, subs, rows, 2, tile, size), lambda i: (i, 0, own_at, 0, 0, 0)),
        pl.BlockSpec((1, subs, MAXS, 2, tile, size), lambda i: (i, 0, rim_at, 0, 0, 0)),
        pl.BlockSpec((1, subs, rows, 2, tile, size), lambda i: (i, 0, part, 0, 0, 0)),
        lines,
        lines,
        lines,
        whole(2 * size, 2 * size),
    ]
    operands = [own, rim, factors, shift, turn_cos, turn_sin, inner]
    scratch = [
        pltpu.VMEM((subs, 2, rows, tile, size), BF16),
        pltpu.VMEM((rows * tile, 2 * size), BF16),
    ]
    if finish:
        total = rows + sum(piece.shape[0] for piece in before)
        in_specs += [pl.BlockSpec(memory_space=pltpu.SMEM), whole(2 * size, 2 * size)]
        in_specs += [whole(*piece.shape) for piece in before]
        operands += [mine, outer, *before]
        out_specs = [whole(2, total, width)] * groups
        out_shape = [jax.ShapeDtypeStruct((2, total, width), BF16)] * groups
        scratch += [
            pltpu.VMEM((rows, 2, size, size), BF16),
            pltpu.VMEM((2 * size * (total + 1), LANES), F32),
        ]
    else:
        out_specs = pl.BlockSpec((rows, 2, tile, size), lambda i: (0, 0, i, 0))
        out_shape = jax.ShapeDtypeStruct((rows, 2, size, size), BF16)
    return pl.pallas_call(
        functools.partial(image_kernel, len(before), finish),
        grid=(size // tile,),
        in_specs=in_specs,
        out_specs=out_specs,
        out_shape=out_shape,
        scratch_shapes=scratch,
        compiler_params=pltpu.CompilerParams(vmem_limit_bytes=VMEM),
        name="image_rows",
    )(*operands)


def place_kernel(mine_ref, *refs):
    pieces, o_ref = refs[:-1], refs[-1]
    rows = pieces[0].shape[1]
    groups = len(pieces) // 2
    for half in range(2):
        for k in range(groups):
            line = (mine_ref[0] ^ k) * 2 * rows + half * rows
            o_ref[0, pl.ds(pl.multiple_of(line, rows), rows), :] = pieces[half * groups + k][0]


def place_rows(mine, pieces):
    _, rows, width = pieces[0].shape
    return pl.pallas_call(
        place_kernel,
        grid=(2,),
        in_specs=[pl.BlockSpec(memory_space=pltpu.SMEM)]
        + [pl.BlockSpec((1, rows, width), lambda i: (i, 0, 0))] * len(pieces),
        out_specs=pl.BlockSpec((1, rows * len(pieces), width), lambda i: (i, 0, 0)),
        out_shape=jax.ShapeDtypeStruct((2, rows * len(pieces), width), BF16),
        compiler_params=pltpu.CompilerParams(vmem_limit_bytes=VMEM),
        name="place_rows",
    )(mine, *pieces)


def on_device(raw_echo, range_phase, kappa, doppler, migration):
    _, _, range_len, pulse_dev = raw_echo.shape
    puls, subs = lax.axis_size("pul"), lax.axis_size("sub")
    blocks = puls * subs
    rows = range_len // blocks
    half = rows // 2
    pulse_len = pulse_dev * puls
    size = math.isqrt(pulse_len)
    sub_index = lax.axis_index("sub")
    mine = sub_index.reshape(1).astype(jnp.int32)
    middle = range_middle(range_phase, math.isqrt(range_len))
    echo = raw_echo.reshape(2, range_len, pulse_dev)

    def spread(sent):
        got = lax.all_to_all(sent, ("pul", "sub"), 0, 0, tiled=True)
        return got.reshape((puls, subs) + sent.shape[1:])

    def swap(pieces):
        sent = [
            lax.ppermute(pieces[k], "sub", [(i, i ^ k) for i in range(subs)])
            for k in range(subs - 1, 0, -1)
        ]
        return [pieces[0]] + sent[::-1]

    width = pulse_dev // 2
    (sent,) = range_compress(echo, middle, 0, width, blocks, 1)
    sent, echo = lax.optimization_barrier((sent, echo))
    first = spread(sent)
    sent_low, sent_high = range_compress(echo, middle, 1, width, blocks, 2)
    own_shift = lax.dynamic_slice_in_dim(migration, sub_index, 1, 0)
    shift = own_shift.reshape(size, size).T
    phase = jnp.swapaxes(doppler.reshape(subs, size, size), 1, 2) * (0.5 / math.pi)
    own_kappa = lax.dynamic_slice_in_dim(kappa, sub_index * rows, rows, 0)
    factors = azimuth_factors(own_kappa, phase)
    first, sent_low, factors, shift = lax.optimization_barrier((first, sent_low, factors, shift))
    got_low = spread(sent_low)
    got_low, sent_high = lax.optimization_barrier((got_low, sent_high))
    got_high = spread(sent_high)
    low, edge = doppler_forward(first, got_low, 0, half, size, True)
    place = lambda block: (block % subs) * puls + block // subs
    pairs = [(place(block), place(block - 1)) for block in range(1, blocks)]
    rim = lax.ppermute(edge, ("sub", "pul"), pairs)
    top = image_rows(low, 0, MAXS, low, 1, factors, 0, shift, None, subs, [])
    got_high, top = lax.optimization_barrier((got_high, top))
    (high,) = doppler_forward(first, got_high, 1, half, size, False)
    pieces = image_rows(low, 1, MAXS, high, 0, factors, 1, shift, mine, subs, [top])
    upper = swap(pieces)
    pieces = image_rows(high, 0, half, rim, 0, factors, 1, shift, mine, subs, [])
    lower = swap(pieces)
    return place_rows(mine, upper + lower)


def solution(mesh):
    placed = (P(None, "sub", None, "pul"), P(), P("pul"), P(), P("pul", None))
    return jax.shard_map(
        on_device, mesh=mesh, in_specs=placed, out_specs=P(None, "pul", "sub"), check_vma=False
    )
```

```python
import functools
import math

import jax
import jax.numpy as jnp
import numpy as np
from jax import lax
from jax.experimental import pallas as pl
from jax.experimental.pallas import tpu as pltpu
from jax.sharding import PartitionSpec as P

MAXS = 8
RBLK = 32
LANES = 128
RANGE_UNROLL = 16
TILE = 64
VMEM = 56 * 1024 * 1024
F32 = jnp.float32
BF16 = jnp.bfloat16


def realified(table):
    return np.block([[table.real, -table.imag], [table.imag, table.real]])


def unit_table(rows, cols, length, direction):
    product = np.outer(np.asarray(rows), np.asarray(cols)) % length
    return np.exp(direction * 2j * np.pi * product / length)


def as_bf16(table):
    return np.asarray(table, np.float32).astype(BF16)


def middle_kernel(phase_ref, wave_ref, o_ref):
    cosine, sine = turns(phase_ref[...])
    size = phase_ref.shape[1] // 2
    lane = lax.broadcasted_iota(jnp.int32, sine.shape, 1)
    sine = jnp.where(lane < size, sine, -sine)
    for k2 in range(o_ref.shape[0]):
        wave = wave_ref[k2].astype(F32)
        left = wave * cosine[k2 : k2 + 1] + pltpu.roll(wave, size, 1) * sine[k2 : k2 + 1]
        o_ref[k2] = lax.dot_general(
            left.astype(BF16),
            wave_ref[k2],
            (((1,), (1,)), ((), ())),
            preferred_element_type=F32,
        ).astype(BF16)


def range_middle(range_phase, size):
    length = size * size
    k2 = np.arange(size)[:, None, None]
    j1 = np.arange(size)[None, :, None]
    k1 = np.arange(size)[None, None, :]
    wave = np.exp(2j * np.pi * ((j1 * (k2 + size * k1)) % length) / length) / size
    wave = as_bf16(np.stack([realified(wave[k]) for k in range(size)]))
    phase = range_phase.reshape(size, size).T * (0.5 / math.pi)
    group = 32
    block = pl.BlockSpec((group, 2 * size, 2 * size), lambda i: (i, 0, 0))
    return pl.pallas_call(
        middle_kernel,
        grid=(size // group,),
        in_specs=[pl.BlockSpec((group, 2 * size), lambda i: (i, 0)), block],
        out_specs=block,
        out_shape=jax.ShapeDtypeStruct(wave.shape, BF16),
        compiler_params=pltpu.CompilerParams(vmem_limit_bytes=VMEM),
        name="range_middle",
    )(jnp.concatenate([phase, phase], axis=1), wave)


def range_kernel(size, splits, x_ref, w_ref, t_ref, v_ref, *refs):
    outs, (one, two) = refs[:splits], refs[splits:]
    halves = x_ref.shape[2] // LANES
    both = 2 * size
    pitch = size + 1

    def lanes(h):
        return slice(h * LANES, (h + 1) * LANES)

    def cast(step, carry):
        for u in range(4):
            line = step * 4 + u
            for h in range(halves):
                for c in range(2):
                    one[h, pl.ds((c * size + line) * pitch, size), :] = x_ref[
                        c, pl.ds(pl.multiple_of(line * size, size), size), lanes(h)
                    ].astype(F32)
        return carry

    lax.fori_loop(0, size // 4, cast, 0)

    def strided(source, target, table):
        def body(step, carry):
            for u in range(RANGE_UNROLL):
                j1 = step * RANGE_UNROLL + u
                value = jnp.concatenate(
                    [source[h, pl.ds(j1, both, stride=pitch), :] for h in range(halves)], axis=1
                ).astype(BF16)
                out = jnp.dot(table, value, preferred_element_type=F32)
                for h in range(halves):
                    target[h, pl.ds(j1, both, stride=pitch), :] = out[:, lanes(h)]
            return carry

        lax.fori_loop(0, size // RANGE_UNROLL, body, 0)

    strided(one, two, w_ref[...])

    def inner(step, carry):
        for u in range(RANGE_UNROLL):
            k2 = step * RANGE_UNROLL + u
            value = jnp.concatenate(
                [
                    jnp.concatenate(
                        [two[h, pl.ds((c * size + k2) * pitch, size), :] for c in range(2)], axis=0
                    )
                    for h in range(halves)
                ],
                axis=1,
            ).astype(BF16)
            out = jnp.dot(t_ref[k2], value, preferred_element_type=F32)
            for h in range(halves):
                for d in range(2):
                    one[h, pl.ds((d * size + k2) * pitch, size), :] = out[
                        d * size : (d + 1) * size, lanes(h)
                    ]
        return carry

    lax.fori_loop(0, size // RANGE_UNROLL, inner, 0)
    strided(one, two, v_ref[...])
    rows = outs[0].shape[2]
    pieces = size // rows

    def give(step, carry):
        for u in range(4):
            line = step * 4 + u
            for piece in range(pieces):
                block = line * (pieces // splits) + piece // splits
                for d in range(2):
                    for h in range(halves):
                        outs[piece % splits][block, d, :, lanes(h)] = two[
                            h, pl.ds((d * size + line) * pitch + piece * rows, rows), :
                        ].astype(BF16)
        return carry

    lax.fori_loop(0, size // 4, give, 0)


def range_compress(echo, middle, chunk, width, blocks, splits):
    length = echo.shape[1]
    size = math.isqrt(length)
    index = np.arange(size)
    forward = as_bf16(realified(unit_table(index, index, size, -1)))
    backward = as_bf16(realified(unit_table(index, index, size, 1)))
    rows = length // blocks // splits
    whole = lambda *shape: pl.BlockSpec(shape, lambda i: (0,) * len(shape))
    scratch = pltpu.VMEM((width // LANES, 2 * (length + size), LANES), F32)
    return pl.pallas_call(
        functools.partial(range_kernel, size, splits),
        grid=(1,),
        in_specs=[
            pl.BlockSpec((2, length, width), lambda i: (0, 0, chunk)),
            whole(2 * size, 2 * size),
            whole(size, 2 * size, 2 * size),
            whole(2 * size, 2 * size),
        ],
        out_specs=[whole(blocks, 2, rows, width)] * splits,
        out_shape=[jax.ShapeDtypeStruct((blocks, 2, rows, width), BF16)] * splits,
        scratch_shapes=[scratch, scratch],
        compiler_params=pltpu.CompilerParams(vmem_limit_bytes=VMEM),
        name="range_compress",
    )(echo, forward, middle, backward)


def doppler_kernel(rows, first, rest, w_ref, cos_ref, sin_ref, u_ref, o_ref, *refs):
    held = refs[-1]
    sources = first.shape[0]
    size = cos_ref.shape[0]
    lines = size // sources
    early = first.shape[4] // LANES
    pitch = rows + 1

    def cast(source, carry):
        for line in range(lines):
            for c in range(2):
                part, at = (first, line) if line < early else (rest, line - early)
                value = part[source, 0, c, :, at * LANES : (at + 1) * LANES]
                base = (c * lines + line) * sources
                held[pl.ds((base + source) * pitch, rows), :] = value.astype(F32)
        return carry

    lax.fori_loop(0, sources, cast, 0)

    def pair(first_row):
        value = jnp.concatenate(
            [held[pl.ds(first_row + i, 2 * size, stride=pitch), :] for i in range(2)], axis=1
        ).astype(BF16)
        first = jnp.dot(w_ref[...], value, preferred_element_type=F32)
        stacked = []
        for i in range(2):
            real = first[:size, i * LANES : (i + 1) * LANES]
            imag = first[size:, i * LANES : (i + 1) * LANES]
            stacked.append(
                jnp.concatenate(
                    [
                        real * cos_ref[...] - imag * sin_ref[...],
                        real * sin_ref[...] + imag * cos_ref[...],
                    ],
                    axis=1,
                ).astype(BF16)
            )
        second = jnp.dot(
            jnp.concatenate(stacked, axis=0), u_ref[...], preferred_element_type=F32
        ).astype(BF16)
        for i in range(2):
            for d in range(2):
                for tile in range(size // TILE):
                    line = i * size + tile * TILE
                    value = second[line : line + TILE, d * LANES : (d + 1) * LANES]
                    o_ref[tile, 0, first_row + i, d] = value

    for first_row in range(0, rows, 2):
        pair(first_row)
    for rim in refs[:-1]:
        rim[:, 0] = o_ref[:, 0, :MAXS]


def doppler_tables(size, direction):
    index = np.arange(size)
    table = unit_table(index, index, size, direction)
    turn = unit_table(index, index, size * size, direction) / size
    return table, turn.real.astype(np.float32), turn.imag.astype(np.float32)


def doppler_forward(first, rest, part, rows, size, with_rim):
    sources, subs, _, _, width = rest.shape
    table, turn_cos, turn_sin = doppler_tables(size, -1)
    lines = size // sources
    order = np.asarray(
        [lines * source + line for line in range(lines) for source in range(sources)]
    )
    outer = as_bf16(realified(table[:, order]))
    inner = as_bf16(realified(table).T)
    whole = lambda *shape: pl.BlockSpec(shape, lambda i: (0,) * len(shape))
    heights = [rows, MAXS] if with_rim else [rows]
    return pl.pallas_call(
        functools.partial(doppler_kernel, rows),
        grid=(subs,),
        in_specs=[
            pl.BlockSpec(
                (sources, 1, 2, rows, first.shape[4]), lambda i: (0, i, 0, part, 0)
            ),
            pl.BlockSpec((sources, 1, 2, rows, width), lambda i: (0, i, 0, 0, 0)),
            whole(2 * size, 2 * size),
            whole(size, size),
            whole(size, size),
            whole(2 * size, 2 * size),
        ],
        out_specs=[
            pl.BlockSpec((size // TILE, 1, height, 2, TILE, size), lambda i: (0, i, 0, 0, 0, 0))
            for height in heights
        ],
        out_shape=[
            jax.ShapeDtypeStruct((size // TILE, subs, height, 2, TILE, size), BF16)
            for height in heights
        ],
        scratch_shapes=[pltpu.VMEM((2 * size * (rows + 1), LANES), F32)],
        compiler_params=pltpu.CompilerParams(vmem_limit_bytes=VMEM),
        name="doppler_forward",
    )(first, rest, outer, turn_cos, turn_sin, inner)


def turn_polynomials():
    nodes = 0.25 * (1 - np.cos((np.arange(64) + 0.5) * np.pi / 64)) / 2
    roots = np.sqrt(nodes)
    sine = np.polynomial.polynomial.polyfit(nodes, np.sin(2 * np.pi * roots) / roots, 6)
    cosine = np.polynomial.polynomial.polyfit(nodes, np.cos(2 * np.pi * roots), 6)
    return [round(float(v), 7) for v in sine], [round(float(v), 7) for v in cosine]


def turns(cycles):
    sine_terms, cosine_terms = turn_polynomials()
    part = cycles - jnp.floor(cycles + 0.5)
    square = part * part
    sine = jnp.full_like(square, sine_terms[-1])
    cosine = jnp.full_like(square, cosine_terms[-1])
    for term in reversed(sine_terms[:-1]):
        sine = sine * square + term
    for term in reversed(cosine_terms[:-1]):
        cosine = cosine * square + term
    return cosine, sine * part


def factor_kernel(kappa_ref, phase_ref, o_ref):
    def body(step, carry):
        for u in range(2):
            row = step * 2 + u
            for tile in range(o_ref.shape[0]):
                cosine, sine = turns(kappa_ref[row] * phase_ref[0, tile * TILE : (tile + 1) * TILE])
                o_ref[tile, 0, row, 0] = cosine.astype(BF16)
                o_ref[tile, 0, row, 1] = sine.astype(BF16)
        return carry

    lax.fori_loop(0, o_ref.shape[2] // 2, body, 0)


def azimuth_factors(kappa, phase):
    subs, size, _ = phase.shape
    rows = kappa.shape[0]
    return pl.pallas_call(
        factor_kernel,
        grid=(subs,),
        in_specs=[
            pl.BlockSpec(memory_space=pltpu.SMEM),
            pl.BlockSpec((1, size, size), lambda i: (i, 0, 0)),
        ],
        out_specs=pl.BlockSpec(
            (size // TILE, 1, rows, 2, TILE, size), lambda i: (0, i, 0, 0, 0, 0)
        ),
        out_shape=jax.ShapeDtypeStruct((size // TILE, subs, rows, 2, TILE, size), BF16),
        compiler_params=pltpu.CompilerParams(vmem_limit_bytes=VMEM),
        name="azimuth_factors",
    )(kappa, phase)


def image_kernel(earlier, finish, *refs):
    own, rim, factor_ref, shift_ref, cos_ref, sin_ref, u_ref = refs[:7]
    refs = refs[7:]
    if finish:
        mine_ref, w_ref = refs[:2]
        before, refs = refs[2 : 2 + earlier], refs[2 + earlier :]
        outs, (moved, summed, middle, turned) = refs[:-4], refs[-4:]
    else:
        (out, moved, summed) = refs
    step = pl.program_id(0)
    _, subs, rows, _, tile, size = own.shape
    shift = shift_ref[...]
    bits = [((shift >> k) & 1).astype(F32).astype(BF16) > 0.5 for k in range(4)]

    def aperture(index, carry):
        for d in range(2):
            values = [own[0, index, r, d] for r in range(rows)]
            values += [rim[0, index, r, d] for r in range(MAXS)]
            four = [jnp.where(bits[2], values[r + 4], values[r]) for r in range(rows + 3)]
            two = [jnp.where(bits[1], four[r + 2], four[r]) for r in range(rows + 1)]
            one = [jnp.where(bits[0], two[r + 1], two[r]) for r in range(rows)]
            for r in range(rows):
                moved[index, d, r] = jnp.where(bits[3], values[r + 8], one[r])
        return carry

    lax.fori_loop(0, subs, aperture, 0)

    def row_sum(turn, carry):
        for u in range(8):
            row = turn * 8 + u
            real = jnp.zeros((tile, size), F32)
            imag = jnp.zeros((tile, size), F32)
            for index in range(subs):
                cosine = factor_ref[0, index, row, 0].astype(F32)
                sine = factor_ref[0, index, row, 1].astype(F32)
                a, b = moved[index, 0, row].astype(F32), moved[index, 1, row].astype(F32)
                real = real + (a * cosine - b * sine)
                imag = imag + (a * sine + b * cosine)
            summed[pl.ds(pl.multiple_of(row * tile, tile), tile), :] = jnp.concatenate(
                [real, imag], axis=1
            ).astype(BF16)
        return carry

    lax.fori_loop(0, rows // 8, row_sum, 0)
    first = jnp.dot(summed[...], u_ref[...], preferred_element_type=F32)
    for r in range(rows):
        real = first[r * tile : (r + 1) * tile, :size]
        imag = first[r * tile : (r + 1) * tile, size:]
        real, imag = (
            (real * cos_ref[...] - imag * sin_ref[...]).astype(BF16),
            (real * sin_ref[...] + imag * cos_ref[...]).astype(BF16),
        )
        if finish:
            where = pl.ds(pl.multiple_of(step * tile, tile), tile)
            middle[r, 0, where, :] = real
            middle[r, 1, where, :] = imag
        else:
            out[r, 0] = real
            out[r, 1] = imag

    if not finish:
        return

    @pl.when(step == pl.num_programs(0) - 1)
    def _():
        held = [(ref, r) for ref in list(before) + [middle] for r in range(ref.shape[0])]
        pitch = len(held) + 1
        for at in range(0, len(held), 2):
            value = jnp.concatenate(
                [
                    jnp.concatenate([ref[r, c] for c in range(2)], axis=0)
                    for ref, r in held[at : at + 2]
                ],
                axis=1,
            )
            result = jnp.dot(w_ref[...], value, preferred_element_type=F32)
            for i in range(2):
                turned[pl.ds(at + i, 2 * size, stride=pitch), :] = result[
                    :, i * LANES : (i + 1) * LANES
                ]
        per_group = size // len(outs)
        for k, piece in enumerate(outs):
            group = mine_ref[0] ^ k
            for d in range(2):
                for j in range(per_group):
                    line = (d * size + group * per_group + j) * pitch
                    piece[d, :, j * LANES : (j + 1) * LANES] = turned[
                        pl.ds(line, len(held)), :
                    ].astype(BF16)


def image_rows(own, own_at, rows, rim, rim_at, factors, part, shift, mine, groups, before):
    _, subs, _, _, tile, size = own.shape
    finish = mine is not None
    table, turn_cos, turn_sin = doppler_tables(size, 1)
    outer = as_bf16(realified(table))
    inner = as_bf16(realified(table).T)
    whole = lambda *shape: pl.BlockSpec(shape, lambda i: (0,) * len(shape))
    lines = pl.BlockSpec((tile, size), lambda i: (i, 0))
    width = size * size // groups
    in_specs = [
        pl.BlockSpec((1, subs, rows, 2, tile, size), lambda i: (i, 0, own_at, 0, 0, 0)),
        pl.BlockSpec((1, subs, MAXS, 2, tile, size), lambda i: (i, 0, rim_at, 0, 0, 0)),
        pl.BlockSpec((1, subs, rows, 2, tile, size), lambda i: (i, 0, part, 0, 0, 0)),
        lines,
        lines,
        lines,
        whole(2 * size, 2 * size),
    ]
    operands = [own, rim, factors, shift, turn_cos, turn_sin, inner]
    scratch = [
        pltpu.VMEM((subs, 2, rows, tile, size), BF16),
        pltpu.VMEM((rows * tile, 2 * size), BF16),
    ]
    if finish:
        total = rows + sum(piece.shape[0] for piece in before)
        in_specs += [pl.BlockSpec(memory_space=pltpu.SMEM), whole(2 * size, 2 * size)]
        in_specs += [whole(*piece.shape) for piece in before]
        operands += [mine, outer, *before]
        out_specs = [whole(2, total, width)] * groups
        out_shape = [jax.ShapeDtypeStruct((2, total, width), BF16)] * groups
        scratch += [
            pltpu.VMEM((rows, 2, size, size), BF16),
            pltpu.VMEM((2 * size * (total + 1), LANES), F32),
        ]
    else:
        out_specs = pl.BlockSpec((rows, 2, tile, size), lambda i: (0, 0, i, 0))
        out_shape = jax.ShapeDtypeStruct((rows, 2, size, size), BF16)
    return pl.pallas_call(
        functools.partial(image_kernel, len(before), finish),
        grid=(size // tile,),
        in_specs=in_specs,
        out_specs=out_specs,
        out_shape=out_shape,
        scratch_shapes=scratch,
        compiler_params=pltpu.CompilerParams(vmem_limit_bytes=VMEM),
        name="image_rows",
    )(*operands)


def place_kernel(mine_ref, *refs):
    pieces, o_ref = refs[:-1], refs[-1]
    rows = pieces[0].shape[1]
    groups = len(pieces) // 2
    for half in range(2):
        for k in range(groups):
            line = (mine_ref[0] ^ k) * 2 * rows + half * rows
            o_ref[0, pl.ds(pl.multiple_of(line, rows), rows), :] = pieces[half * groups + k][0]


def place_rows(mine, pieces):
    _, rows, width = pieces[0].shape
    return pl.pallas_call(
        place_kernel,
        grid=(2,),
        in_specs=[pl.BlockSpec(memory_space=pltpu.SMEM)]
        + [pl.BlockSpec((1, rows, width), lambda i: (i, 0, 0))] * len(pieces),
        out_specs=pl.BlockSpec((1, rows * len(pieces), width), lambda i: (i, 0, 0)),
        out_shape=jax.ShapeDtypeStruct((2, rows * len(pieces), width), BF16),
        compiler_params=pltpu.CompilerParams(vmem_limit_bytes=VMEM),
        name="place_rows",
    )(mine, *pieces)


def on_device(raw_echo, range_phase, kappa, doppler, migration):
    _, _, range_len, pulse_dev = raw_echo.shape
    puls, subs = lax.axis_size("pul"), lax.axis_size("sub")
    blocks = puls * subs
    rows = range_len // blocks
    half = rows // 2
    pulse_len = pulse_dev * puls
    size = math.isqrt(pulse_len)
    sub_index = lax.axis_index("sub")
    mine = sub_index.reshape(1).astype(jnp.int32)
    middle = range_middle(range_phase, math.isqrt(range_len))
    echo = raw_echo.reshape(2, range_len, pulse_dev)

    def spread(sent):
        got = lax.all_to_all(sent, ("pul", "sub"), 0, 0, tiled=True)
        return got.reshape((puls, subs) + sent.shape[1:])

    def swap(pieces):
        sent = [
            lax.ppermute(pieces[k], "sub", [(i, i ^ k) for i in range(subs)])
            for k in range(subs - 1, 0, -1)
        ]
        return [pieces[0]] + sent[::-1]

    width = pulse_dev // 2
    (sent,) = range_compress(echo, middle, 0, width, blocks, 1)
    sent, echo = lax.optimization_barrier((sent, echo))
    first = spread(sent)
    sent_low, sent_high = range_compress(echo, middle, 1, width, blocks, 2)
    own_shift = lax.dynamic_slice_in_dim(migration, sub_index, 1, 0)
    shift = own_shift.reshape(size, size).T
    phase = jnp.swapaxes(doppler.reshape(subs, size, size), 1, 2) * (0.5 / math.pi)
    own_kappa = lax.dynamic_slice_in_dim(kappa, sub_index * rows, rows, 0)
    factors = azimuth_factors(own_kappa, phase)
    first, sent_low, factors, shift = lax.optimization_barrier((first, sent_low, factors, shift))
    got_low = spread(sent_low)
    got_low, sent_high = lax.optimization_barrier((got_low, sent_high))
    got_high = spread(sent_high)
    low, edge = doppler_forward(first, got_low, 0, half, size, True)
    place = lambda block: (block % subs) * puls + block // subs
    pairs = [(place(block), place(block - 1)) for block in range(1, blocks)]
    rim = lax.ppermute(edge, ("sub", "pul"), pairs)
    top = image_rows(low, 0, MAXS, low, 1, factors, 0, shift, None, subs, [])
    got_high, top = lax.optimization_barrier((got_high, top))
    (high,) = doppler_forward(first, got_high, 1, half, size, False)
    pieces = image_rows(low, 1, MAXS, high, 0, factors, 1, shift, mine, subs, [top])
    upper = swap(pieces)
    pieces = image_rows(high, 0, half, rim, 0, factors, 1, shift, mine, subs, [])
    lower = swap(pieces)
    return place_rows(mine, upper + lower)


def solution(mesh):
    placed = (P(None, "sub", None, "pul"), P(), P("pul"), P(), P("pul", None))
    return jax.shard_map(
        on_device, mesh=mesh, in_specs=placed, out_specs=P(None, "pul", "sub"), check_vma=False
    )
```
